256 devices in a mesh: row: 8 (over y, x_hi), phi: 32 (over x_lo, z, core).
Axes of the slice: x: 4 (x_hi: 2, x_lo: 2; x = x_hi * 2 + x_lo), y: 4, z: 8, core: 2. Of those that a mesh axis runs over, the one named last changes fastest.
Arguments:
- density: float32 [32, 16, 8192], P('row', None, 'phi'), may hold values from 0.5 to 2
- momentum: float32 [3, 32, 16, 8192], P(None, 'row', None, 'phi'), may hold values from -3 to 3
- field: float32 [3, 32, 16, 8192], P(None, 'row', None, 'phi'), may hold values from -3 to 3
- shift: int32 [32], P('row'), may hold values from 0 to 8191
- frac: float32 [32], P('row'), may hold values from 0 to 1
Outputs:
- density_next: float32 [32, 16, 8192], P('row', None, 'phi')
- momentum_next: float32 [3, 32, 16, 8192], P(None, 'row', None, 'phi')
- field_next: float32 [3, 32, 16, 8192], P(None, 'row', None, 'phi')
The draws below stay inside these ranges and needn't reach their ends.
Inputs may be any that keep to these rules, and one draw needn't show every extreme that they name: The shift of a radial column applies to every vertical and azimuthal cell of that column.
All inputs are finite; a program needn't handle non-finite values.
Results may differ from the reference program's by a relative error of at most 0.00002.
Values sent between devices are 32-bit elements; how exact they have to be, the bound alone decides.
A program may use at most 64 MiB of HBM per device.

```python
import jax
import jax.numpy as jnp
from jax import lax

NZ = 16
NX = 32
NY = 8192


def plant(entries, stream_key, least, high):
    index_at = [jax.random.randint(jax.random.fold_in(stream_key, axis), (), 0, length) for axis, length in enumerate(entries.shape)]
    longest = entries.shape.index(max(entries.shape))
    beside = index_at[:longest] + [(index_at[longest] + 1) % entries.shape[longest]] + index_at[longest + 1:]
    return entries.at[tuple(index_at)].set(least).at[tuple(beside)].set(high)


def block_scale(rng, dims, shards, smallest, high):
    level, own = 1.0, jax.random.fold_in(rng, 6)
    for axis_at, parts in shards:
        steps = jnp.exp(jax.random.uniform(jax.random.fold_in(own, axis_at), (parts,), jnp.float32, smallest / len(shards), high / len(shards)))
        level = level * jnp.repeat(steps, dims[axis_at] // parts).reshape([-1 if axis == axis_at else 1 for axis in range(len(dims))])
    return level


def scatter_about(stream_key, extent, deviation, reach, cuts=(), kind=jnp.bfloat16):
    values = jax.random.normal(stream_key, extent, jnp.float32) * deviation
    if len(cuts) > 0:
        values = block_scale(stream_key, extent, cuts, -0.22, 0.18) * values
    return jnp.clip(values, min=-reach, max=reach).astype(kind)


def setup_inputs(seed: int = 0) -> dict:
    splits = jax.random.split(jax.random.key(seed), 6)
    density = jnp.clip(0.5 + 1.5 * jax.random.uniform(splits[0], (NX, NZ, NY), jnp.float32) ** block_scale(splits[0], (NX, NZ, NY), ((0, 8), (2, 32)), -0.2, 0.2), 0.5, 2.0)
    momentum = scatter_about(splits[1], (3, NX, NZ, NY), 0.5, 3.0, ((1, 8), (3, 32)), jnp.float32)
    field = scatter_about(splits[2], (3, NX, NZ, NY), 0.5, 3.0, ((1, 8), (3, 32)), jnp.float32)
    shift = plant(jax.random.randint(splits[3], (NX,), 0, NY), jax.random.fold_in(splits[3], 1), 0, NY - 1).astype(jnp.int32)
    frac = jnp.clip(1.0 * jax.random.uniform(splits[4], (NX,), jnp.float32) ** block_scale(splits[4], (NX,), ((0, 8),), -0.2, 0.2), 0.0, 1.0)
    return {"density": density, "momentum": momentum, "field": field, "shift": shift, "frac": frac}


TIME_STEP = 0.025
SOUND_SQUARED = 1.0
ORBIT_FREQ = 1.0
SHEAR_RATE = 1.5
NORMAL_AXES = (0, 2, 1)

def from_lower(values, axis_dim):
    return jnp.roll(values, 1, axis_dim)

def from_upper(values, axis_dim):
    return jnp.roll(values, -1, axis_dim)

def exit_update(values, fraction, axis_dim):
    upcoming = jnp.roll(values, -1, axis_dim)
    previous = jnp.roll(values, 1, axis_dim)
    further = jnp.roll(values, -2, axis_dim)
    interface = 7.0 / 12.0 * (values + upcoming) - 1.0 / 12.0 * (previous + further)
    interface = jnp.clip(interface, jnp.minimum(values, upcoming), jnp.maximum(values, upcoming))
    left_face = jnp.roll(interface, 1, axis_dim)
    curvature = 6.0 * (values - 0.5 * (interface + left_face))
    outgoing = fraction * (interface - 0.5 * fraction * (interface - left_face - (1.0 - 2.0 / 3.0 * fraction) * curvature))
    return values - outgoing + jnp.roll(outgoing, 1, axis_dim)

def face_flux(density, momenta, normal_field, centred, normal_dir):
    axis_dim = NORMAL_AXES[normal_dir]

    def state_of(picker):
        fields = [picker(entry) for entry in centred]
        fields[normal_dir] = normal_field
        return (picker(density), [picker(entry) for entry in momenta], fields)
    lower_state = state_of(lambda values: from_lower(values, axis_dim))
    upper_state = state_of(lambda values: values)

    def physical(state):
        dens, moms, fields = state
        veloc = [entry / dens for entry in moms]
        magnetic = 0.5 * (fields[0] * fields[0] + fields[1] * fields[1] + fields[2] * fields[2])
        flux_moms = [moms[comp] * veloc[normal_dir] - fields[normal_dir] * fields[comp] for comp in range(3)]
        flux_moms[normal_dir] = flux_moms[normal_dir] + (dens * SOUND_SQUARED + magnetic)
        flux_fields = [fields[comp] * veloc[normal_dir] - fields[normal_dir] * veloc[comp] for comp in range(3)]
        speed = jnp.abs(veloc[normal_dir]) + jnp.sqrt(SOUND_SQUARED + 2.0 * magnetic / dens)
        return (moms[normal_dir], flux_moms, flux_fields, speed)
    lower_flux = physical(lower_state)
    upper_flux = physical(upper_state)
    fastest = jnp.maximum(lower_flux[3], upper_flux[3])

    def blend(flux_low, flux_up, cons_low, cons_up):
        return 0.5 * (flux_low + flux_up) - 0.5 * fastest * (cons_up - cons_low)
    mass = blend(lower_flux[0], upper_flux[0], lower_state[0], upper_state[0])
    moms = [blend(lower_flux[1][comp], upper_flux[1][comp], lower_state[1][comp], upper_state[1][comp]) for comp in range(3)]
    fields = [blend(lower_flux[2][comp], upper_flux[2][comp], lower_state[2][comp], upper_state[2][comp]) for comp in range(3)]
    return (mass, moms, fields)

def godunov(extended):
    density = extended[0]
    momenta = [extended[1], extended[2], extended[3]]
    faces = [extended[4], extended[5], extended[6]]
    centred = [0.5 * (faces[comp] + from_upper(faces[comp], NORMAL_AXES[comp])) for comp in range(3)]
    fluxes = [face_flux(density, momenta, faces[direc], centred, direc) for direc in range(3)]
    edge_z = 0.25 * (-fluxes[0][2][1] - from_lower(fluxes[0][2][1], 2) + fluxes[1][2][0] + from_lower(fluxes[1][2][0], 0))
    edge_y = 0.25 * (fluxes[0][2][2] + from_lower(fluxes[0][2][2], 1) - fluxes[2][2][0] - from_lower(fluxes[2][2][0], 0))
    edge_x = 0.25 * (-fluxes[1][2][2] - from_lower(fluxes[1][2][2], 1) + fluxes[2][2][1] + from_lower(fluxes[2][2][1], 2))

    def rise(values, axis_dim):
        return from_upper(values, axis_dim) - values
    field_x = faces[0] - TIME_STEP * (rise(edge_z, 2) - rise(edge_y, 1))
    field_y = faces[1] - TIME_STEP * (rise(edge_x, 1) - rise(edge_z, 0))
    field_z = faces[2] - TIME_STEP * (rise(edge_y, 0) - rise(edge_x, 2))

    def divergence(pieces):
        total = rise(pieces[0], NORMAL_AXES[0])
        total = total + rise(pieces[1], NORMAL_AXES[1])
        return total + rise(pieces[2], NORMAL_AXES[2])
    new_density = density - TIME_STEP * divergence([fluxes[direc][0] for direc in range(3)])
    new_moms = [momenta[comp] - TIME_STEP * divergence([fluxes[direc][1][comp] for direc in range(3)]) for comp in range(3)]
    new_moms[0] = new_moms[0] + TIME_STEP * 2.0 * ORBIT_FREQ * momenta[1]
    new_moms[1] = new_moms[1] - TIME_STEP * (2.0 - SHEAR_RATE) * ORBIT_FREQ * momenta[0]
    stacked = jnp.stack([new_density, new_moms[0], new_moms[1], new_moms[2], field_x, field_y, field_z])
    return stacked[:, 2:-2, :, 2:-2]

def reference(density, momentum, field, shift, frac):
    fields_all = jnp.concatenate([density[None], momentum, field], 0)
    columns = jnp.moveaxis(fields_all, 1, 0)

    def remap_column(packed):
        column, offset, fraction = packed
        exited = exit_update(column, fraction, 2)
        return jnp.roll(exited, offset, 2)
    remapped = jnp.moveaxis(lax.map(remap_column, (columns, shift, frac)), 0, 1)
    padded = jnp.pad(remapped, ((0, 0), (2, 2), (0, 0), (2, 2)), mode='wrap')

    def update_block(start):
        piece = lax.dynamic_slice_in_dim(padded, start, 6, 1)
        return godunov(piece)
    starts = jnp.arange(NX // 2, dtype=jnp.int32) * 2
    blocks = lax.map(update_block, starts)
    result = jnp.moveaxis(blocks, 0, 1).reshape(7, NX, NZ, NY)
    return (result[0], result[1:4], result[4:7])
```

```python
import functools

import jax
import jax.numpy as jnp
from jax import lax
from jax.experimental import pallas as pl
from jax.experimental.pallas import tpu as pltpu
from jax.sharding import PartitionSpec as P

MESH = pl.DeviceIdType.MESH
TIME_STEP = 0.025
SOUND_SQUARED = 1.0
ORBIT_FREQ = 1.0
SHEAR_RATE = 1.5

ROWS = 8
PHI = 32
NZ = 16
LANES = 128
FIELDS = 7
TILE = 16
RING = PHI * TILE
CHUNKS = 2 * PHI
COLUMNS = ((0, 3), (1, 2))
GROUP = 8


def ring_exit(q, fraction, lane):
    def upward(values, by):
        turned = pltpu.roll(values, LANES - by, 2)
        return jnp.where(lane >= LANES - by, turned[1:], turned[:-1])

    def downward(values):
        turned = pltpu.roll(values, 1, 2)
        return jnp.where(lane == 0, turned[:-1], turned[1:])

    here = q[1:-1]
    one = upward(q, 1)[1:]
    two = upward(q, 2)[1:]
    before = downward(q)[:-1]
    face = 7.0 / 12.0 * (here + one) - 1.0 / 12.0 * (before + two)
    face = jnp.clip(face, jnp.minimum(here, one), jnp.maximum(here, one))
    left = jnp.concatenate([pltpu.roll(face[:1], 1, 2), downward(face)], 0)
    curvature = 6.0 * (here - 0.5 * (face + left))
    outgoing = fraction * (
        face - 0.5 * fraction * (face - left - (1.0 - 2.0 / 3.0 * fraction) * curvature)
    )
    return here[1:] - outgoing[1:] + downward(outgoing)


def transport_kernel(
    shift_ref, frac_ref, dens_ref, mom_ref, fld_ref, own_ref, halo_ref, five_ref,
    send_f, recv_f, send_b, turned, five, sem_fs, sem_fr, sem_bs, sem_br, sem_xs, sem_xr,
):
    row = lax.axis_index("row")
    me = lax.axis_index("phi")
    above = (lax.rem(row + 1, ROWS), me)
    below = (lax.rem(row + ROWS - 1, ROWS), me)
    barrier = pltpu.get_barrier_semaphore()

    def greet(t, carry):
        pl.semaphore_signal(
            barrier, inc=1, device_id=(row, lax.rem(me + t, PHI)), device_id_type=MESH
        )
        return carry

    lax.fori_loop(1, PHI, greet, 0)
    pl.semaphore_signal(barrier, inc=1, device_id=above, device_id_type=MESH)
    pl.semaphore_signal(barrier, inc=1, device_id=below, device_id_type=MESH)

    def source(f, x, zs, ys):
        if f == 0:
            return dens_ref[x, zs, ys]
        if f < 4:
            return mom_ref[f - 1, x, zs, ys]
        return fld_ref[f - 4, x, zs, ys]

    def arrange(stage):
        for side in range(2):
            for half in range(2):
                for zt in range(2):
                    for f in range(8):
                        first = (side * NZ + 8 * zt) * TILE + half * 8 + f
                        if f < FIELDS:
                            block = source(
                                f, COLUMNS[stage][side], slice(8 * zt, 8 * zt + 8),
                                slice(LANES * half, LANES * half + LANES),
                            )
                        else:
                            block = jnp.zeros((8, LANES), jnp.float32)
                        send_f[stage, pl.ds(first, 8, stride=TILE), :] = block

    def rows_of(index):
        return pl.ds(pl.multiple_of(index * TILE, TILE), TILE)

    def spread(stage, src, dst, send_sem, recv_sem):
        def one(t, carry):
            to = lax.rem(me + t, PHI)
            pltpu.make_async_remote_copy(
                src_ref=src.at[stage, rows_of(to), :],
                dst_ref=dst.at[stage, rows_of(me), :],
                send_sem=send_sem.at[stage],
                recv_sem=recv_sem.at[stage],
                device_id=(row, to),
                device_id_type=MESH,
            ).start()
            return carry

        lax.fori_loop(1, PHI, one, 0)

    def settle(stage, buffer, sem):
        part = buffer.at[stage, pl.ds(0, RING - TILE), :]
        pltpu.make_async_copy(part, part, sem.at[stage]).wait()

    arrange(0)
    pl.semaphore_wait(barrier, PHI - 1 + 2)
    spread(0, send_f, recv_f, sem_fs, sem_fr)
    arrange(1)
    spread(1, send_f, recv_f, sem_fs, sem_fr)

    lane = lax.broadcasted_iota(jnp.int32, (1, 8, LANES), 2)
    sub = lax.broadcasted_iota(jnp.int32, (1, 8, LANES), 1)
    spot = lane - 3 * sub

    def turn(stage):
        column = jnp.where(me < NZ, COLUMNS[stage][0], COLUMNS[stage][1])
        cells = shift_ref[column]
        fraction = frac_ref[column]
        blocks = lax.shift_right_logical(cells, 7)
        inner = cells & (LANES - 1)
        recv_f[stage, rows_of(me), :] = send_f[stage, rows_of(me), :]

        def leave(i, carry):
            first = i * 2 * GROUP

            def chunk(c):
                at = lax.rem(c + CHUNKS, CHUNKS)
                return recv_f[stage, pl.ds(pl.multiple_of(at * 8, 8), 8), :].reshape(1, 8, LANES)

            body = recv_f[stage, pl.ds(pl.multiple_of(first * 8, 8), 16 * GROUP), :]
            q = jnp.concatenate(
                [chunk(first - 2), chunk(first - 1), body.reshape(2 * GROUP, 8, LANES),
                 chunk(first + 2 * GROUP)], 0
            )
            exited = ring_exit(q, fraction, lane)
            rolled = pltpu.roll(exited, inner, 2)
            turned[pl.ds(first + 2, 2 * GROUP)] = rolled
            turned[pl.ds(first + 66, 2 * GROUP)] = rolled
            return carry

        lax.fori_loop(0, PHI // GROUP, leave, 0)
        turned[0:2] = turned[64:66]
        turned[130] = turned[66]

        def place(i, carry):
            first = i * 2 * GROUP
            start = first + 64 - blocks
            window = jnp.stack([turned[start + j] for j in range(2 * GROUP + 3)])
            out = jnp.where(lane >= inner, window[1:], window[:-1])
            pairs = out.reshape(GROUP + 1, 2, 8, LANES)
            lower = pairs[:GROUP, 0]
            main = out[1:-1].reshape(GROUP, 2, 8, LANES)
            upper = pairs[1:, 1]
            ends = jnp.where(lane == 0, pltpu.roll(lower, 1, 2), pltpu.roll(upper, 1, 2))
            packed = jnp.where(spot == 0, ends[:, :, 0:1], 0.0)
            packed = jnp.where(spot == 1, ends[:, :, 1:2], packed)
            packed = jnp.where(spot == 2, ends[:, :, 2:3], packed)
            packed = jnp.sum(packed, axis=1, keepdims=True)
            low = jnp.where(sub == 7, packed, main[:, 0])
            both = jnp.concatenate([low[:, None], main[:, 1:]], 1)
            send_b[stage, pl.ds(pl.multiple_of(first * 8, 8), 16 * GROUP), :] = both.reshape(
                16 * GROUP, LANES
            )
            return carry

        lax.fori_loop(0, PHI // GROUP, place, 0)

    for stage in range(2):
        settle(stage, recv_f, sem_fr)
        turn(stage)
        spread(stage, send_b, own_ref, sem_bs, sem_br)
        own_ref[stage, rows_of(me), :] = send_b[stage, rows_of(me), :]

    half = NZ * TILE
    settle(0, own_ref, sem_br)
    upward = pltpu.make_async_remote_copy(
        src_ref=own_ref.at[0, pl.ds(half, half), :], dst_ref=halo_ref.at[0],
        send_sem=sem_xs.at[0], recv_sem=sem_xr.at[0], device_id=above, device_id_type=MESH,
    )
    downward = pltpu.make_async_remote_copy(
        src_ref=own_ref.at[0, pl.ds(0, half), :], dst_ref=halo_ref.at[1],
        send_sem=sem_xs.at[1], recv_sem=sem_xr.at[1], device_id=below, device_id_type=MESH,
    )
    upward.start()
    downward.start()
    settle(1, own_ref, sem_br)
    for k in range(2):
        ends = own_ref[1, pl.ds(8 * 2 * k + 7, 8, stride=2 * TILE), :]
        five[k, :, 0:LANES] = own_ref[1, pl.ds(16 * k + 4, 8, stride=2 * TILE), :]
        five[k, :, LANES:2 * LANES] = own_ref[1, pl.ds(16 * k + 12, 8, stride=2 * TILE), :]
        five[k, :, 2 * LANES:] = pltpu.roll(ends, LANES - 13, 1)
    second = pltpu.make_async_remote_copy(
        src_ref=five, dst_ref=five_ref,
        send_sem=sem_xs.at[2], recv_sem=sem_xr.at[2], device_id=below, device_id_type=MESH,
    )
    second.start()
    upward.wait()
    downward.wait()
    second.wait()
    for stage in range(2):
        settle(stage, send_f, sem_fs)
        settle(stage, send_b, sem_bs)


def up_z(values):
    return jnp.concatenate([values[1:2], pltpu.roll(values[0:1], 7, 1)], 0)


def low_z(values):
    return jnp.concatenate([pltpu.roll(values[1:2], 1, 1), values[0:1]], 0)


def up_y(values):
    return pltpu.roll(values, values.shape[2] - 1, 2)


def low_y(values):
    return pltpu.roll(values, 1, 2)


def same(values):
    return values


def cell_of(state, upper_bx):
    rho, mx, my, mz, bx, by, bz = state
    inv = 1.0 / rho
    m = (mx, my, mz)
    v = (mx * inv, my * inv, mz * inv)
    b = (0.5 * (bx + upper_bx), 0.5 * (by + up_y(by)), 0.5 * (bz + up_z(bz)))
    return dict(rho=rho, inv=inv, m=m, v=v, b=b, faces=(bx, by, bz))


def side_of(cell, n):
    t, u = [c for c in range(3) if c != n]
    m, v, b = cell["m"], cell["v"], cell["b"]
    across = b[t] * b[t] + b[u] * b[u]
    return dict(
        m=m, v=v, b=b, inv=cell["inv"], rho=cell["rho"],
        base=SOUND_SQUARED + across * cell["inv"],
        speed=jnp.abs(v[n]),
        push=m[n] * v[n] + (cell["rho"] * SOUND_SQUARED + 0.5 * across),
    )


def face_flux(low, high, normal, n, moved, wanted):
    others = [c for c in range(3) if c != n]
    square = normal * normal

    def fast(side, shifted):
        return shifted(side["speed"]) + jnp.sqrt(shifted(side["base"]) + square * shifted(side["inv"]))

    fastest = jnp.maximum(fast(low, moved), fast(high, same))
    result = {}

    def blend(flux_low, flux_high, state_low, state_high):
        return (flux_low + flux_high) - fastest * (state_high - state_low)

    if "mass" in wanted:
        result["mass"] = blend(moved(low["m"][n]), high["m"][n], moved(low["rho"]), high["rho"])
    if "m" in wanted:
        moms = [None] * 3
        moms[n] = blend(moved(low["push"]), high["push"], moved(low["m"][n]), high["m"][n]) - square
        for t in others:
            moms[t] = blend(
                moved(low["m"][t] * low["v"][n]), high["m"][t] * high["v"][n],
                moved(low["m"][t]), high["m"][t],
            ) - normal * (moved(low["b"][t]) + high["b"][t])
        result["m"] = moms
    for t in others:
        if ("b", t) in wanted:
            result["b", t] = blend(
                moved(low["b"][t] * low["v"][n]), high["b"][t] * high["v"][n],
                moved(low["b"][t]), high["b"][t],
            ) - normal * (moved(low["v"][t]) + high["v"][t])
    return result


def godunov(load, five, store):
    states = {i: load(i) for i in range(-1, 5)}
    cells = {}
    for i in range(-1, 5):
        cells[i] = cell_of(states[i], states[i + 1][4] if i < 4 else five)
    xs = {}
    for i in range(0, 5):
        if i == 0:
            low = side_of(cells[-1], 0)
        high = side_of(cells[i], 0)
        xs[i] = face_flux(low, high, cells[i]["faces"][0], 0, same, ("mass", "m", ("b", 1), ("b", 2)))
        low = high
    ys, zs = {}, {}
    for i in range(-1, 5):
        inner = 0 <= i < 4
        side = side_of(cells[i], 1)
        ys[i] = face_flux(
            side, side, cells[i]["faces"][1], 1, low_y,
            ("mass", "m", ("b", 0), ("b", 2)) if inner else (("b", 0),),
        )
        side = side_of(cells[i], 2)
        zs[i] = face_flux(
            side, side, cells[i]["faces"][2], 2, low_z,
            ("mass", "m", ("b", 0), ("b", 1)) if inner else (("b", 0),),
        )
    edge_z, edge_y, edge_x = {}, {}, {}
    for i in range(0, 5):
        edge_z[i] = ys[i]["b", 0] + ys[i - 1]["b", 0] - (xs[i]["b", 1] + low_y(xs[i]["b", 1]))
        edge_y[i] = xs[i]["b", 2] + low_z(xs[i]["b", 2]) - (zs[i]["b", 0] + zs[i - 1]["b", 0])
        if i < 4:
            edge_x[i] = zs[i]["b", 1] + low_y(zs[i]["b", 1]) - (ys[i]["b", 2] + low_z(ys[i]["b", 2]))
    step = 0.5 * TIME_STEP
    edge_step = 0.125 * TIME_STEP
    for i in range(0, 4):
        cell = cells[i]

        def divergence(pick):
            y, z = pick(ys[i]), pick(zs[i])
            return (pick(xs[i + 1]) - pick(xs[i])) + (up_y(y) - y) + (up_z(z) - z)

        store(0, i, cell["rho"] - step * divergence(lambda flux: flux["mass"]))
        new = [cell["m"][c] - step * divergence(lambda flux: flux["m"][c]) for c in range(3)]
        new[0] = new[0] + TIME_STEP * 2.0 * ORBIT_FREQ * cell["m"][1]
        new[1] = new[1] - TIME_STEP * (2.0 - SHEAR_RATE) * ORBIT_FREQ * cell["m"][0]
        for c in range(3):
            store(1 + c, i, new[c])
        bx, by, bz = cell["faces"]
        ez, ey, ex = edge_z[i], edge_y[i], edge_x[i]
        store(4, i, bx - edge_step * ((up_y(ez) - ez) - (up_z(ey) - ey)))
        store(5, i, by - edge_step * ((up_z(ex) - ex) - (edge_z[i + 1] - ez)))
        store(6, i, bz - edge_step * ((edge_y[i + 1] - ey) - (up_y(ex) - ex)))


def update_kernel(own_ref, halo_ref, five_ref, dens_ref, mom_ref, fld_ref, weave):
    def load(i):
        if i == -1:
            part, base = halo_ref.at[0], 0
        elif i == 4:
            part, base = halo_ref.at[1], 0
        else:
            part = own_ref.at[0 if i in (0, 3) else 1]
            base = 0 if i < 2 else NZ * TILE
        result = []
        for f in range(FIELDS):
            pieces = []
            for k in range(2):
                first = base + k * TILE
                ends = part[pl.ds(first + 7, 8, stride=2 * TILE), :]
                pieces.append(jnp.concatenate([
                    part[pl.ds(first + f, 8, stride=2 * TILE), :],
                    part[pl.ds(first + 8 + f, 8, stride=2 * TILE), :],
                    pltpu.roll(ends, LANES - (3 * f + 1), 1),
                ], 1)[None])
            result.append(jnp.concatenate(pieces, 0))
        return result

    def store(f, i, values):
        for half in range(2):
            for k in range(2):
                weave[f, i, half, pl.ds(k, 8, stride=2), :] = values[k, :, half * LANES:half * LANES + LANES]
            block = weave[f, i, half]
            ys = slice(half * LANES, half * LANES + LANES)
            if f == 0:
                dens_ref[i, :, ys] = block
            elif f < 4:
                mom_ref[f - 1, i, :, ys] = block
            else:
                fld_ref[f - 4, i, :, ys] = block

    godunov(load, five_ref[...], store)


def body(density, momentum, field, shift, frac):
    vmem = pl.BlockSpec(memory_space=pltpu.VMEM)
    smem = pl.BlockSpec(memory_space=pltpu.SMEM)
    f32 = jnp.float32
    own, halo, five = pl.pallas_call(
        transport_kernel,
        out_shape=(
            jax.ShapeDtypeStruct((2, RING, LANES), f32),
            jax.ShapeDtypeStruct((2, NZ * TILE, LANES), f32),
            jax.ShapeDtypeStruct((2, 8, 3 * LANES), f32),
        ),
        in_specs=[smem, smem, vmem, vmem, vmem],
        out_specs=(vmem, vmem, vmem),
        scratch_shapes=[
            pltpu.VMEM((2, RING, LANES), f32),
            pltpu.VMEM((2, RING, LANES), f32),
            pltpu.VMEM((2, RING, LANES), f32),
            pltpu.VMEM((131, 8, LANES), f32),
            pltpu.VMEM((2, 8, 3 * LANES), f32),
            pltpu.SemaphoreType.DMA((2,)),
            pltpu.SemaphoreType.DMA((2,)),
            pltpu.SemaphoreType.DMA((2,)),
            pltpu.SemaphoreType.DMA((2,)),
            pltpu.SemaphoreType.DMA((3,)),
            pltpu.SemaphoreType.DMA((3,)),
        ],
        compiler_params=pltpu.CompilerParams(
            collective_id=0, has_side_effects=True, vmem_limit_bytes=32 * 2**20
        ),
        name="transport",
    )(shift, frac, density, momentum, field)
    return pl.pallas_call(
        update_kernel,
        out_shape=(
            jax.ShapeDtypeStruct(density.shape, f32),
            jax.ShapeDtypeStruct(momentum.shape, f32),
            jax.ShapeDtypeStruct(field.shape, f32),
        ),
        in_specs=[vmem, vmem, vmem],
        out_specs=(vmem, vmem, vmem),
        scratch_shapes=[pltpu.VMEM((FIELDS, 4, 2, NZ, LANES), f32)],
        compiler_params=pltpu.CompilerParams(vmem_limit_bytes=32 * 2**20),
        name="update",
    )(own, halo, five)


def solution(mesh):
    return jax.shard_map(
        body,
        mesh=mesh,
        in_specs=(
            P("row", None, "phi"),
            P(None, "row", None, "phi"),
            P(None, "row", None, "phi"),
            P("row"),
            P("row"),
        ),
        out_specs=(P("row", None, "phi"), P(None, "row", None, "phi"), P(None, "row", None, "phi")),
        check_vma=False,
    )
```

```python
import functools

import jax
import jax.numpy as jnp
from jax import lax
from jax.experimental import pallas as pl
from jax.experimental.pallas import tpu as pltpu
from jax.sharding import PartitionSpec as P

MESH = pl.DeviceIdType.MESH
TIME_STEP = 0.025
SOUND_SQUARED = 1.0
ORBIT_FREQ = 1.0
SHEAR_RATE = 1.5

ROWS = 8
PHI = 32
NZ = 16
LANES = 128
FIELDS = 7
PARTS = 4
COLUMNS = ((0, 3), (0, 3), (1, 2), (1, 2))
FIRST = (0, 4, 0, 4)
TILE = 8
RING = PHI * TILE
HALF = RING // 2
OUT_ROWS = (8, 8, 8, 6)
UPPER = (4, 4, 4, 3)
BACK_ROWS = (8, 8, 8, 7)


def after(values, by):
    return jnp.concatenate([values[by:], values[:by]], 0)


def ring_exit(q, fraction, lane, later, earlier):
    def upward(by):
        turned = pltpu.roll(q, LANES - by, 2)
        return jnp.where(lane >= LANES - by, later(turned), turned)

    def downward(values):
        turned = pltpu.roll(values, 1, 2)
        return jnp.where(lane == 0, earlier(turned), turned)

    one, two, before = upward(1), upward(2), downward(q)
    face = 7.0 / 12.0 * (q + one) - 1.0 / 12.0 * (before + two)
    face = jnp.clip(face, jnp.minimum(q, one), jnp.maximum(q, one))
    left = downward(face)
    curvature = 6.0 * (q - 0.5 * (face + left))
    outgoing = fraction * (
        face - 0.5 * fraction * (face - left - (1.0 - 2.0 / 3.0 * fraction) * curvature)
    )
    return q - outgoing + downward(outgoing)


def step_kernel(
    shift_hbm, frac_hbm, dens_hbm, mom_hbm, fld_hbm, dens_out, mom_out, fld_out,
    shift_ref, frac_ref, dens_ref, mom_ref, fld_ref, send_f, recv_f, send_b, turned, tails, own_ref, halo_ref,
    five, five_ref, weave, sem_in, sem_fs, sem_fr, sem_bs, sem_br, sem_xs, sem_xr, sem_out,
):
    row = lax.axis_index("row")
    me = lax.axis_index("phi")
    above = (lax.rem(row + 1, ROWS), me)
    below = (lax.rem(row + ROWS - 1, ROWS), me)
    barrier = pltpu.get_barrier_semaphore()

    def greet(t, carry):
        pl.semaphore_signal(
            barrier, inc=1, device_id=(row, lax.rem(me + t, PHI)), device_id_type=MESH
        )
        return carry

    lax.fori_loop(1, PHI, greet, 0)
    pl.semaphore_signal(barrier, inc=1, device_id=above, device_id_type=MESH)
    pl.semaphore_signal(barrier, inc=1, device_id=below, device_id_type=MESH)

    fetches = [
        pltpu.make_async_copy(src, dst, sem_in.at[k])
        for k, (src, dst) in enumerate((
            (dens_hbm, dens_ref), (mom_hbm, mom_ref), (fld_hbm, fld_ref),
            (shift_hbm, shift_ref), (frac_hbm, frac_ref),
        ))
    ]
    for fetch in fetches:
        fetch.start()

    def source(f, x, zs, ys):
        if f == 0:
            return dens_ref[x, zs, ys]
        if f < 4:
            return mom_ref[f - 1, x, zs, ys]
        return fld_ref[f - 4, x, zs, ys]

    def arrange(part):
        for side in range(2):
            for half in range(2):
                for zt in range(2):
                    for j in range(3 if part == 3 else 4):
                        f, x = FIRST[part] + j, COLUMNS[part][side]
                        if f == FIELDS:
                            f, x = 4, 1
                        block = source(
                            f, x, slice(8 * zt, 8 * zt + 8), slice(LANES * half, LANES * half + LANES)
                        )
                        first = (side * NZ + 8 * zt) * TILE + half * UPPER[part] + j
                        send_f[part, pl.ds(first, 8, stride=TILE), :] = block

    def rows_of(index, count=TILE):
        return pl.ds(pl.multiple_of(index * TILE, TILE), count)

    def spread(part, count, src, dst, send_sem, recv_sem):
        def one(t, carry):
            to = lax.rem(me + t, PHI)
            pltpu.make_async_remote_copy(
                src_ref=src.at[part, rows_of(to, count), :],
                dst_ref=dst.at[part, rows_of(me, count), :],
                send_sem=send_sem.at[part],
                recv_sem=recv_sem.at[part],
                device_id=(row, to),
                device_id_type=MESH,
            ).start()
            return carry

        lax.fori_loop(1, PHI, one, 0)

    def settle(part, count, buffer, sem):
        rows = buffer.at[part, pl.ds(0, (PHI - 1) * count), :]
        pltpu.make_async_copy(rows, rows, sem.at[part]).wait()

    def send_out(part):
        spread(part, OUT_ROWS[part], send_f, recv_f, sem_fs, sem_fr)

    lane = lax.broadcasted_iota(jnp.int32, (1, 8, LANES), 2)
    sub = lax.broadcasted_iota(jnp.int32, (1, 8, LANES), 1)
    lower = sub < 4
    spare = (sub & 3) == 3

    def later(values):
        return pltpu.roll(jnp.where(lower, after(values, 1), values), 4, 1)

    def earlier(values):
        return pltpu.roll(jnp.where(lower, values, after(values, -1)), 4, 1)

    def turn(part):
        settle(part, OUT_ROWS[part], recv_f, sem_fr)
        recv_f[part, rows_of(me), :] = send_f[part, rows_of(me), :]
        column = jnp.where(me < NZ, COLUMNS[part][0], COLUMNS[part][1])
        fraction = frac_ref[column]
        cells = shift_ref[column]
        inner = cells & (LANES - 1)
        if part == 1:
            fraction = jnp.where(spare, frac_ref[1], fraction)
            cells_1 = shift_ref[1]
            inner_1 = cells_1 & (LANES - 1)
        q = recv_f[part].reshape(PHI, 8, LANES)
        if part == 3:
            q = jnp.where(lower, q, pltpu.roll(q, 1, 1))
        exited = ring_exit(q, fraction, lane, later, earlier)
        rolled = pltpu.roll(exited, inner, 2)
        if part == 1:
            rolled = jnp.where(spare, pltpu.roll(exited, inner_1, 2), rolled)
        turned[0:PHI] = rolled
        turned[PHI:] = rolled

        def moved(amount):
            start = PHI - lax.shift_right_logical(amount, 8)
            blocks = jnp.stack([turned[start + j] for j in range(PHI)])
            return jnp.where((amount & LANES) == 0, blocks, earlier(blocks))

        out, split = moved(cells), inner
        if part == 1:
            out, split = jnp.where(spare, moved(cells_1), out), jnp.where(spare, inner_1, inner)
        out = jnp.where(lane >= split, out, earlier(out))
        ends = pltpu.roll(out, 1, 2)
        ends = jnp.where(lane == 0, pltpu.roll(after(ends, -1), 4, 1), after(ends, 1))
        spot = jnp.where(sub < (3 if part == 3 else 4), lane - 3 * (sub + FIRST[part]), -1)
        packed = jnp.where(spot == 0, ends[:, :, 0:1], 0.0)
        packed = jnp.where(spot == 1, ends[:, :, 1:2], packed)
        packed = jnp.where(spot == 2, ends[:, :, 2:3], packed)
        packed = jnp.sum(packed, axis=1, keepdims=True)
        if FIRST[part] == 0:
            tails[...] = jnp.broadcast_to(packed, tails.shape)
        else:
            packed = packed + tails[...]
            if part == 1:
                out = jnp.where((sub == 7) & (me < NZ), pltpu.roll(out, 4, 1), out)
            out = jnp.where(sub == 3, packed, out)
        send_b[part] = out.reshape(RING, LANES)
        spread(part, BACK_ROWS[part], send_b, own_ref, sem_bs, sem_br)
        own_ref[part, rows_of(me), :] = send_b[part, rows_of(me), :]

    def swap_of(k, src, dst, to):
        return pltpu.make_async_remote_copy(
            src_ref=src, dst_ref=dst, send_sem=sem_xs.at[k], recv_sem=sem_xr.at[k],
            device_id=to, device_id_type=MESH,
        )

    def swap(part):
        settle(part, BACK_ROWS[part], own_ref, sem_br)
        both = [
            swap_of(2 * part, own_ref.at[part, pl.ds(HALF, HALF), :], halo_ref.at[0, part], above),
            swap_of(2 * part + 1, own_ref.at[part, pl.ds(0, HALF), :], halo_ref.at[1, part], below),
        ]
        for each in both:
            each.start()
        return both

    for fetch in fetches:
        fetch.wait()
    arrange(0)
    pl.semaphore_wait(barrier, PHI - 1 + 2)
    send_out(0)
    arrange(1)
    send_out(1)
    arrange(2)
    send_out(2)
    arrange(3)
    turn(0)
    turn(1)
    send_out(3)
    turn(2)
    swaps = swap(0) + swap(1)
    for k in range(2):
        five[k] = own_ref[1, pl.ds(HALF + TILE * k + 7, 8, stride=2 * TILE), :]
    swaps.append(swap_of(4, five, five_ref, below))
    swaps[-1].start()
    turn(3)

    def gather(rows, ends, f):
        pieces = []
        for k in range(2):
            halves = [part[pl.ds(base + k * TILE + r, 8, stride=2 * TILE), :] for part, base, r in rows]
            part, base = ends
            tail = part[pl.ds(base + k * TILE + 3, 8, stride=2 * TILE), :]
            pieces.append(
                jnp.concatenate(halves + [pltpu.roll(tail, LANES - (3 * f + 1), 1)], 1)[None]
            )
        return jnp.concatenate(pieces, 0)

    def load(i):
        if i in (-1, 4):
            parts, base = [halo_ref.at[0 if i < 0 else 1, k] for k in range(2)], 0
        else:
            parts = [own_ref.at[(0 if i in (0, 3) else 2) + k] for k in range(2)]
            base = 0 if i < 2 else HALF
        return [
            gather([(parts[f // 4], base, f % 4), (parts[f // 4], base, 4 + f % 4)], (parts[1], base), f)
            for f in range(FIELDS)
        ]

    def load_one():
        part = own_ref.at[1]
        return gather([(part, 0, 7), (part, HALF, 7)], (part, 0), FIELDS)

    def load_five():
        part = halo_ref.at[1, 1]
        pieces = []
        for k in range(2):
            lower_half = part[pl.ds(k * TILE + 7, 8, stride=2 * TILE), :]
            tail = part[pl.ds(k * TILE + 3, 8, stride=2 * TILE), :]
            pieces.append(
                jnp.concatenate([lower_half, five_ref[k], pltpu.roll(tail, LANES - 22, 1)], 1)[None]
            )
        return jnp.concatenate(pieces, 0)

    step = Step(load, {1: load_one, 5: load_five})
    writes = []

    def finish(i, fields):
        for f in fields:
            values = step.result(f, i)
            for side in range(2):
                for k in range(2):
                    weave[f, i, side, pl.ds(k, 8, stride=2), :] = values[
                        k, :, side * LANES:side * LANES + LANES
                    ]
        for side in range(2):
            ys = pl.ds(side * LANES, LANES)
            for src, dst in (
                (weave.at[0, i, side], dens_out.at[i, :, ys]),
                (weave.at[pl.ds(1, 3), i, side], mom_out.at[:, i, :, ys]),
                (weave.at[pl.ds(4, 3), i, side], fld_out.at[:, i, :, ys]),
            ):
                write = pltpu.make_async_copy(src, dst, sem_out.at[len(writes)])
                write.start()
                writes.append(write)

    for each in swaps:
        each.wait()
    step.flux(0, 0)
    step.flux(4, 0)
    for i in (-1, 0, 3, 4):
        step.flux(i, 1)
        step.flux(i, 2)
    settle(2, BACK_ROWS[2], own_ref, sem_br)
    settle(3, BACK_ROWS[3], own_ref, sem_br)
    for i in range(4):
        finish(i, range(FIELDS))
    for part in range(PARTS):
        settle(part, OUT_ROWS[part], send_f, sem_fs)
        settle(part, BACK_ROWS[part], send_b, sem_bs)
    for write in writes:
        write.wait()


def up_z(values):
    return jnp.concatenate([values[1:2], pltpu.roll(values[0:1], 7, 1)], 0)


def low_z(values):
    return jnp.concatenate([pltpu.roll(values[1:2], 1, 1), values[0:1]], 0)


def up_y(values):
    return pltpu.roll(values, values.shape[2] - 1, 2)


def low_y(values):
    return pltpu.roll(values, 1, 2)


def same(values):
    return values


def face_flux(low, high, normal, n, moved, wanted):
    square = normal * normal

    def fast(side, shifted):
        return shifted(side["speed"]) + jnp.sqrt(shifted(side["base"]) + square * shifted(side["inv"]))

    fastest = jnp.maximum(fast(low, moved), fast(high, same))

    def blend(flux_low, flux_high, state_low, state_high):
        return (flux_low + flux_high) - fastest * (state_high - state_low)

    result = {}
    if "m" in wanted:
        result["m"] = [blend(moved(low["m"][n]), high["m"][n], moved(low["rho"]), high["rho"])]
        for t in range(3):
            if t == n:
                part = blend(moved(low["push"]), high["push"], moved(low["m"][n]), high["m"][n]) - square
            else:
                part = blend(
                    moved(low["m"][t] * low["v"][n]), high["m"][t] * high["v"][n],
                    moved(low["m"][t]), high["m"][t],
                ) - normal * (moved(low["b"][t]) + high["b"][t])
            result["m"].append(part)
    for t in range(3):
        if t in wanted:
            result[t] = blend(
                moved(low["b"][t] * low["v"][n]), high["b"][t] * high["v"][n],
                moved(low["b"][t]), high["b"][t],
            ) - normal * (moved(low["v"][t]) + high["v"][t])
    return result


class Step:
    def __init__(self, load, radial):
        self.load, self.radial, self.kept = load, radial, {}

    def keep(self, key, make):
        if key not in self.kept:
            self.kept[key] = make()
        return self.kept[key]

    def state(self, i):
        return self.keep(("state", i), lambda: self.load(i))

    def across(self, i, c):
        def make():
            faces = self.state(i)[4:]
            if c == 0:
                upper = self.radial[i + 1]() if i in (0, 4) else self.state(i + 1)[4]
            else:
                upper = up_y(faces[1]) if c == 1 else up_z(faces[2])
            return 0.5 * (faces[c] + upper)

        return self.keep(("across", i, c), make)

    def cell(self, i):
        def make():
            rho, mx, my, mz = self.state(i)[:4]
            inv = 1.0 / rho
            return dict(rho=rho, inv=inv, m=(mx, my, mz), v=(mx * inv, my * inv, mz * inv))

        return self.keep(("cell", i), make)

    def side(self, i, n):
        def make():
            cell = self.cell(i)
            t, u = [c for c in range(3) if c != n]
            b = {t: self.across(i, t), u: self.across(i, u)}
            square = b[t] * b[t] + b[u] * b[u]
            return dict(
                cell, b=b, base=SOUND_SQUARED + square * cell["inv"], speed=jnp.abs(cell["v"][n]),
                push=cell["m"][n] * cell["v"][n] + (cell["rho"] * SOUND_SQUARED + 0.5 * square),
            )

        return self.keep(("side", i, n), make)

    def flux(self, i, n):
        def make():
            inner = 0 <= i < 4
            normal = self.state(i)[4 + n]
            high = self.side(i, n)
            if n == 0:
                return face_flux(self.side(i - 1, 0), high, normal, 0, same, ("m", 1, 2))
            other = 3 - n
            return face_flux(
                high, high, normal, n, low_y if n == 1 else low_z, ("m", 0, other) if inner else (0,)
            )

        return self.keep(("flux", i, n), make)

    def edge(self, i, c):
        def make():
            if c == 2:
                by = self.flux(i, 0)[1]
                return self.flux(i, 1)[0] + self.flux(i - 1, 1)[0] - (by + low_y(by))
            if c == 1:
                bz = self.flux(i, 0)[2]
                return bz + low_z(bz) - (self.flux(i, 2)[0] + self.flux(i - 1, 2)[0])
            by, bz = self.flux(i, 2)[1], self.flux(i, 1)[2]
            return by + low_y(by) - (bz + low_z(bz))

        return self.keep(("edge", i, c), make)

    def result(self, f, i):
        step, edge_step = 0.5 * TIME_STEP, 0.125 * TIME_STEP
        if f < 4:
            y, z = self.flux(i, 1)["m"][f], self.flux(i, 2)["m"][f]
            total = (self.flux(i + 1, 0)["m"][f] - self.flux(i, 0)["m"][f]) + (up_y(y) - y) + (up_z(z) - z)
            new = self.state(i)[f] - step * total
            if f == 1:
                new = new + TIME_STEP * 2.0 * ORBIT_FREQ * self.state(i)[2]
            if f == 2:
                new = new - TIME_STEP * (2.0 - SHEAR_RATE) * ORBIT_FREQ * self.state(i)[1]
            return new
        if f == 4:
            ez, ey = self.edge(i, 2), self.edge(i, 1)
            curl = (up_y(ez) - ez) - (up_z(ey) - ey)
        elif f == 5:
            ex = self.edge(i, 0)
            curl = (up_z(ex) - ex) - (self.edge(i + 1, 2) - self.edge(i, 2))
        else:
            ex = self.edge(i, 0)
            curl = (self.edge(i + 1, 1) - self.edge(i, 1)) - (up_y(ex) - ex)
        return self.state(i)[f] - edge_step * curl


def pass_kernel(*refs):
    sources, targets, kept, sems = refs[:3], refs[3:6], refs[6:9], refs[9]
    inward = [pltpu.make_async_copy(src, dst, sems.at[0, k]) for k, (src, dst) in enumerate(zip(sources, kept))]
    outward = [pltpu.make_async_copy(src, dst, sems.at[1, k]) for k, (src, dst) in enumerate(zip(kept, targets))]
    for copy in inward:
        copy.start()
    for there, back in zip(inward, outward):
        there.wait()
        back.start()
    for copy in outward:
        copy.wait()


def body(density, momentum, field, shift, frac):
    hbm = pl.BlockSpec(memory_space=pl.ANY)
    f32 = jnp.float32
    shapes = tuple(jax.ShapeDtypeStruct(a.shape, f32) for a in (density, momentum, field))
    results = pl.pallas_call(
        step_kernel,
        out_shape=shapes,
        in_specs=[hbm] * 5,
        out_specs=(hbm,) * 3,
        scratch_shapes=[
            pltpu.SMEM(shift.shape, jnp.int32),
            pltpu.SMEM(frac.shape, f32),
            pltpu.VMEM(density.shape, f32),
            pltpu.VMEM(momentum.shape, f32),
            pltpu.VMEM(field.shape, f32),
            pltpu.VMEM((PARTS, RING, LANES), f32),
            pltpu.VMEM((PARTS, RING, LANES), f32),
            pltpu.VMEM((PARTS, RING, LANES), f32),
            pltpu.VMEM((2 * PHI, 8, LANES), f32),
            pltpu.VMEM((PHI, 8, LANES), f32),
            pltpu.VMEM((PARTS, RING, LANES), f32),
            pltpu.VMEM((2, 2, HALF, LANES), f32),
            pltpu.VMEM((2, 8, LANES), f32),
            pltpu.VMEM((2, 8, LANES), f32),
            pltpu.VMEM((FIELDS, 4, 2, NZ, LANES), f32),
            pltpu.SemaphoreType.DMA((5,)),
            pltpu.SemaphoreType.DMA((PARTS,)),
            pltpu.SemaphoreType.DMA((PARTS,)),
            pltpu.SemaphoreType.DMA((PARTS,)),
            pltpu.SemaphoreType.DMA((PARTS,)),
            pltpu.SemaphoreType.DMA((5,)),
            pltpu.SemaphoreType.DMA((5,)),
            pltpu.SemaphoreType.DMA((24,)),
        ],
        compiler_params=pltpu.CompilerParams(
            collective_id=0, has_side_effects=True, vmem_limit_bytes=56 * 2**20
        ),
        name="step",
    )(shift, frac, density, momentum, field)
    return pl.pallas_call(
        pass_kernel,
        out_shape=shapes,
        in_specs=[hbm] * 3,
        out_specs=(hbm,) * 3,
        scratch_shapes=[pltpu.VMEM(a.shape, f32) for a in shapes] + [pltpu.SemaphoreType.DMA((2, 3))],
        compiler_params=pltpu.CompilerParams(vmem_limit_bytes=56 * 2**20),
        name="hand_on",
    )(*results)


def solution(mesh):
    return jax.shard_map(
        body,
        mesh=mesh,
        in_specs=(
            P("row", None, "phi"),
            P(None, "row", None, "phi"),
            P(None, "row", None, "phi"),
            P("row"),
            P("row"),
        ),
        out_specs=(P("row", None, "phi"), P(None, "row", None, "phi"), P(None, "row", None, "phi")),
        check_vma=False,
    )
```

```python
import functools

import jax
import jax.numpy as jnp
from jax import lax
from jax.experimental import pallas as pl
from jax.experimental.pallas import tpu as pltpu
from jax.sharding import PartitionSpec as P

MESH = pl.DeviceIdType.MESH
TIME_STEP = 0.025
SOUND_SQUARED = 1.0
ORBIT_FREQ = 1.0
SHEAR_RATE = 1.5

ROWS = 8
PHI = 32
NZ = 16
LANES = 128
FIELDS = 7
PARTS = 4
COLUMNS = ((0, 3), (0, 3), (1, 2), (1, 2))
FIRST = (0, 4, 0, 4)
TILE = 8
RING = PHI * TILE
HALF = RING // 2
OUT_ROWS = (8, 8, 8, 6)
UPPER = (4, 4, 4, 3)
BACK_ROWS = (8, 8, 8, 7)


def after(values, by):
    return jnp.concatenate([values[by:], values[:by]], 0)


def ring_exit(q, fraction, lane, later, earlier):
    def upward(by):
        turned = pltpu.roll(q, LANES - by, 2)
        return jnp.where(lane >= LANES - by, later(turned), turned)

    def downward(values):
        turned = pltpu.roll(values, 1, 2)
        return jnp.where(lane == 0, earlier(turned), turned)

    one, two, before = upward(1), upward(2), downward(q)
    face = 7.0 / 12.0 * (q + one) - 1.0 / 12.0 * (before + two)
    face = jnp.clip(face, jnp.minimum(q, one), jnp.maximum(q, one))
    left = downward(face)
    curvature = 6.0 * (q - 0.5 * (face + left))
    outgoing = fraction * (
        face - 0.5 * fraction * (face - left - (1.0 - 2.0 / 3.0 * fraction) * curvature)
    )
    return q - outgoing + downward(outgoing)


def step_kernel(
    shift_hbm, frac_hbm, dens_hbm, mom_hbm, fld_hbm, dens_out, mom_out, fld_out,
    shift_ref, frac_ref, dens_ref, mom_ref, fld_ref, send_f, recv_f, send_b, turned, tails, own_ref, halo_ref,
    five, five_ref, weave, sem_in, sem_fs, sem_fr, sem_bs, sem_br, sem_xs, sem_xr, sem_out,
):
    row = lax.axis_index("row")
    me = lax.axis_index("phi")
    above = (lax.rem(row + 1, ROWS), me)
    below = (lax.rem(row + ROWS - 1, ROWS), me)
    barrier = pltpu.get_barrier_semaphore()

    def partner(i):
        k = i // 4
        dz = 4 + (k + 1) // 2 * (1 - 2 * (k % 2))
        z = lax.rem(me // 2 + dz + 8, 8)
        x = lax.rem(me // 16 + 1 - i // 2 % 2, 2)
        return x * 16 + z * 2 + lax.rem(me + 1 - i % 2, 2)

    def greet(i, carry):
        pl.semaphore_signal(
            barrier, inc=1, device_id=(row, partner(i)), device_id_type=MESH
        )
        return carry

    lax.fori_loop(0, PHI - 1, greet, 0)
    pl.semaphore_signal(barrier, inc=1, device_id=above, device_id_type=MESH)
    pl.semaphore_signal(barrier, inc=1, device_id=below, device_id_type=MESH)

    fetches = [
        pltpu.make_async_copy(src, dst, sem_in.at[k])
        for k, (src, dst) in enumerate((
            (dens_hbm, dens_ref), (mom_hbm, mom_ref), (fld_hbm, fld_ref),
            (shift_hbm, shift_ref), (frac_hbm, frac_ref),
        ))
    ]
    for fetch in fetches:
        fetch.start()

    def source(f, x, zs, ys):
        if f == 0:
            return dens_ref[x, zs, ys]
        if f < 4:
            return mom_ref[f - 1, x, zs, ys]
        return fld_ref[f - 4, x, zs, ys]

    def arrange(part):
        for side in range(2):
            for half in range(2):
                for zt in range(2):
                    for j in range(3 if part == 3 else 4):
                        f, x = FIRST[part] + j, COLUMNS[part][side]
                        if f == FIELDS:
                            f, x = 4, 1
                        block = source(
                            f, x, slice(8 * zt, 8 * zt + 8), slice(LANES * half, LANES * half + LANES)
                        )
                        first = (side * NZ + 8 * zt) * TILE + half * UPPER[part] + j
                        send_f[part, pl.ds(first, 8, stride=TILE), :] = block

    def rows_of(index, count=TILE):
        return pl.ds(pl.multiple_of(index * TILE, TILE), count)

    def spread(part, count, src, dst, send_sem, recv_sem):
        def one(i, carry):
            to = partner(i)
            pltpu.make_async_remote_copy(
                src_ref=src.at[part, rows_of(to, count), :],
                dst_ref=dst.at[part, rows_of(me, count), :],
                send_sem=send_sem.at[part],
                recv_sem=recv_sem.at[part],
                device_id=(row, to),
                device_id_type=MESH,
            ).start()
            return carry

        lax.fori_loop(0, PHI - 1, one, 0)

    def settle(part, count, buffer, sem):
        rows = buffer.at[part, pl.ds(0, (PHI - 1) * count), :]
        pltpu.make_async_copy(rows, rows, sem.at[part]).wait()

    def send_out(part):
        spread(part, OUT_ROWS[part], send_f, recv_f, sem_fs, sem_fr)

    lane = lax.broadcasted_iota(jnp.int32, (1, 8, LANES), 2)
    sub = lax.broadcasted_iota(jnp.int32, (1, 8, LANES), 1)
    lower = sub < 4
    spare = (sub & 3) == 3

    def later(values):
        return pltpu.roll(jnp.where(lower, after(values, 1), values), 4, 1)

    def earlier(values):
        return pltpu.roll(jnp.where(lower, values, after(values, -1)), 4, 1)

    def turn(part):
        settle(part, OUT_ROWS[part], recv_f, sem_fr)
        recv_f[part, rows_of(me), :] = send_f[part, rows_of(me), :]
        column = jnp.where(me < NZ, COLUMNS[part][0], COLUMNS[part][1])
        fraction = frac_ref[column]
        cells = shift_ref[column]
        inner = cells & (LANES - 1)
        if part == 1:
            fraction = jnp.where(spare, frac_ref[1], fraction)
            cells_1 = shift_ref[1]
            inner_1 = cells_1 & (LANES - 1)
        q = recv_f[part].reshape(PHI, 8, LANES)
        if part == 3:
            q = jnp.where(lower, q, pltpu.roll(q, 1, 1))
        exited = ring_exit(q, fraction, lane, later, earlier)
        rolled = pltpu.roll(exited, inner, 2)
        if part == 1:
            rolled = jnp.where(spare, pltpu.roll(exited, inner_1, 2), rolled)
        turned[0:PHI] = rolled
        turned[PHI:] = rolled

        def moved(amount):
            start = PHI - lax.shift_right_logical(amount, 8)
            blocks = jnp.stack([turned[start + j] for j in range(PHI)])
            return jnp.where((amount & LANES) == 0, blocks, earlier(blocks))

        out, split = moved(cells), inner
        if part == 1:
            out, split = jnp.where(spare, moved(cells_1), out), jnp.where(spare, inner_1, inner)
        out = jnp.where(lane >= split, out, earlier(out))
        ends = pltpu.roll(out, 1, 2)
        ends = jnp.where(lane == 0, pltpu.roll(after(ends, -1), 4, 1), after(ends, 1))
        spot = jnp.where(sub < (3 if part == 3 else 4), lane - 3 * (sub + FIRST[part]), -1)
        packed = jnp.where(spot == 0, ends[:, :, 0:1], 0.0)
        packed = jnp.where(spot == 1, ends[:, :, 1:2], packed)
        packed = jnp.where(spot == 2, ends[:, :, 2:3], packed)
        packed = jnp.sum(packed, axis=1, keepdims=True)
        if FIRST[part] == 0:
            tails[...] = jnp.broadcast_to(packed, tails.shape)
        else:
            packed = packed + tails[...]
            if part == 1:
                out = jnp.where((sub == 7) & (me < NZ), pltpu.roll(out, 4, 1), out)
            out = jnp.where(sub == 3, packed, out)
        send_b[part] = out.reshape(RING, LANES)
        spread(part, BACK_ROWS[part], send_b, own_ref, sem_bs, sem_br)
        own_ref[part, rows_of(me), :] = send_b[part, rows_of(me), :]

    def swap_of(k, src, dst, to):
        return pltpu.make_async_remote_copy(
            src_ref=src, dst_ref=dst, send_sem=sem_xs.at[k], recv_sem=sem_xr.at[k],
            device_id=to, device_id_type=MESH,
        )

    def swap(part):
        settle(part, BACK_ROWS[part], own_ref, sem_br)
        both = [
            swap_of(2 * part, own_ref.at[part, pl.ds(HALF, HALF), :], halo_ref.at[0, part], above),
            swap_of(2 * part + 1, own_ref.at[part, pl.ds(0, HALF), :], halo_ref.at[1, part], below),
        ]
        for each in both:
            each.start()
        return both

    for fetch in fetches:
        fetch.wait()
    arrange(0)
    pl.semaphore_wait(barrier, PHI - 1 + 2)
    send_out(0)
    arrange(1)
    send_out(1)
    arrange(2)
    send_out(2)
    arrange(3)
    turn(0)
    send_out(3)
    turn(1)
    turn(2)
    swaps = swap(0)
    turn(3)
    swaps += swap(1)
    for k in range(2):
        five[k] = own_ref[1, pl.ds(HALF + TILE * k + 7, 8, stride=2 * TILE), :]
    swaps.append(swap_of(4, five, five_ref, below))
    swaps[-1].start()

    def gather(rows, ends, f):
        pieces = []
        for k in range(2):
            halves = [part[pl.ds(base + k * TILE + r, 8, stride=2 * TILE), :] for part, base, r in rows]
            part, base = ends
            tail = part[pl.ds(base + k * TILE + 3, 8, stride=2 * TILE), :]
            pieces.append(
                jnp.concatenate(halves + [pltpu.roll(tail, LANES - (3 * f + 1), 1)], 1)[None]
            )
        return jnp.concatenate(pieces, 0)

    def load(i):
        if i in (-1, 4):
            parts, base = [halo_ref.at[0 if i < 0 else 1, k] for k in range(2)], 0
        else:
            parts = [own_ref.at[(0 if i in (0, 3) else 2) + k] for k in range(2)]
            base = 0 if i < 2 else HALF
        return [
            gather([(parts[f // 4], base, f % 4), (parts[f // 4], base, 4 + f % 4)], (parts[1], base), f)
            for f in range(FIELDS)
        ]

    def load_one():
        part = own_ref.at[1]
        return gather([(part, 0, 7), (part, HALF, 7)], (part, 0), FIELDS)

    def load_five():
        part = halo_ref.at[1, 1]
        pieces = []
        for k in range(2):
            lower_half = part[pl.ds(k * TILE + 7, 8, stride=2 * TILE), :]
            tail = part[pl.ds(k * TILE + 3, 8, stride=2 * TILE), :]
            pieces.append(
                jnp.concatenate([lower_half, five_ref[k], pltpu.roll(tail, LANES - 22, 1)], 1)[None]
            )
        return jnp.concatenate(pieces, 0)

    step = Step(load, {1: load_one, 5: load_five})
    writes = []

    def finish(i, fields):
        for f in fields:
            values = step.result(f, i)
            for side in range(2):
                for k in range(2):
                    weave[f, i, side, pl.ds(k, 8, stride=2), :] = values[
                        k, :, side * LANES:side * LANES + LANES
                    ]
        for side in range(2):
            ys = pl.ds(side * LANES, LANES)
            for src, dst in (
                (weave.at[0, i, side], dens_out.at[i, :, ys]),
                (weave.at[pl.ds(1, 3), i, side], mom_out.at[:, i, :, ys]),
                (weave.at[pl.ds(4, 3), i, side], fld_out.at[:, i, :, ys]),
            ):
                write = pltpu.make_async_copy(src, dst, sem_out.at[len(writes)])
                write.start()
                writes.append(write)

    step.flux(0, 1)
    step.flux(0, 2)
    step.side(3, 0)
    settle(2, BACK_ROWS[2], own_ref, sem_br)
    settle(3, BACK_ROWS[3], own_ref, sem_br)
    finish(1, range(FIELDS))
    for i in (2, 3):
        step.flux(i, 0)
    for i in (1, 2):
        step.flux(i, 1)
        step.flux(i, 2)
    for each in swaps:
        each.wait()
    for i in (2, 0, 3):
        finish(i, range(FIELDS))
    for part in range(PARTS):
        settle(part, OUT_ROWS[part], send_f, sem_fs)
        settle(part, BACK_ROWS[part], send_b, sem_bs)
    for write in writes:
        write.wait()


def up_z(values):
    return jnp.concatenate([values[1:2], pltpu.roll(values[0:1], 7, 1)], 0)


def low_z(values):
    return jnp.concatenate([pltpu.roll(values[1:2], 1, 1), values[0:1]], 0)


def up_y(values):
    return pltpu.roll(values, values.shape[2] - 1, 2)


def low_y(values):
    return pltpu.roll(values, 1, 2)


def same(values):
    return values


def face_flux(low, high, normal, n, moved, wanted):
    square = normal * normal

    def fast(side, shifted):
        return shifted(side["speed"]) + jnp.sqrt(shifted(side["base"]) + square * shifted(side["inv"]))

    fastest = jnp.maximum(fast(low, moved), fast(high, same))

    def blend(flux_low, flux_high, state_low, state_high):
        return (flux_low + flux_high) - fastest * (state_high - state_low)

    result = {}
    if "m" in wanted:
        result["m"] = [blend(moved(low["m"][n]), high["m"][n], moved(low["rho"]), high["rho"])]
        for t in range(3):
            if t == n:
                part = blend(moved(low["push"]), high["push"], moved(low["m"][n]), high["m"][n]) - square
            else:
                part = blend(
                    moved(low["m"][t] * low["v"][n]), high["m"][t] * high["v"][n],
                    moved(low["m"][t]), high["m"][t],
                ) - normal * (moved(low["b"][t]) + high["b"][t])
            result["m"].append(part)
    for t in range(3):
        if t in wanted:
            result[t] = blend(
                moved(low["b"][t] * low["v"][n]), high["b"][t] * high["v"][n],
                moved(low["b"][t]), high["b"][t],
            ) - normal * (moved(low["v"][t]) + high["v"][t])
    return result


class Step:
    def __init__(self, load, radial):
        self.load, self.radial, self.kept = load, radial, {}

    def keep(self, key, make):
        if key not in self.kept:
            self.kept[key] = make()
        return self.kept[key]

    def state(self, i):
        return self.keep(("state", i), lambda: self.load(i))

    def across(self, i, c):
        def make():
            faces = self.state(i)[4:]
            if c == 0:
                upper = self.radial[i + 1]() if i in (0, 4) else self.state(i + 1)[4]
            else:
                upper = up_y(faces[1]) if c == 1 else up_z(faces[2])
            return 0.5 * (faces[c] + upper)

        return self.keep(("across", i, c), make)

    def cell(self, i):
        def make():
            rho, mx, my, mz = self.state(i)[:4]
            inv = 1.0 / rho
            return dict(rho=rho, inv=inv, m=(mx, my, mz), v=(mx * inv, my * inv, mz * inv))

        return self.keep(("cell", i), make)

    def side(self, i, n):
        def make():
            cell = self.cell(i)
            t, u = [c for c in range(3) if c != n]
            b = {t: self.across(i, t), u: self.across(i, u)}
            square = b[t] * b[t] + b[u] * b[u]
            return dict(
                cell, b=b, base=SOUND_SQUARED + square * cell["inv"], speed=jnp.abs(cell["v"][n]),
                push=cell["m"][n] * cell["v"][n] + (cell["rho"] * SOUND_SQUARED + 0.5 * square),
            )

        return self.keep(("side", i, n), make)

    def flux(self, i, n):
        def make():
            inner = 0 <= i < 4
            normal = self.state(i)[4 + n]
            high = self.side(i, n)
            if n == 0:
                return face_flux(self.side(i - 1, 0), high, normal, 0, same, ("m", 1, 2))
            other = 3 - n
            return face_flux(
                high, high, normal, n, low_y if n == 1 else low_z, ("m", 0, other) if inner else (0,)
            )

        return self.keep(("flux", i, n), make)

    def edge(self, i, c):
        def make():
            if c == 2:
                by = self.flux(i, 0)[1]
                return self.flux(i, 1)[0] + self.flux(i - 1, 1)[0] - (by + low_y(by))
            if c == 1:
                bz = self.flux(i, 0)[2]
                return bz + low_z(bz) - (self.flux(i, 2)[0] + self.flux(i - 1, 2)[0])
            by, bz = self.flux(i, 2)[1], self.flux(i, 1)[2]
            return by + low_y(by) - (bz + low_z(bz))

        return self.keep(("edge", i, c), make)

    def result(self, f, i):
        step, edge_step = 0.5 * TIME_STEP, 0.125 * TIME_STEP
        if f < 4:
            y, z = self.flux(i, 1)["m"][f], self.flux(i, 2)["m"][f]
            total = (self.flux(i + 1, 0)["m"][f] - self.flux(i, 0)["m"][f]) + (up_y(y) - y) + (up_z(z) - z)
            new = self.state(i)[f] - step * total
            if f == 1:
                new = new + TIME_STEP * 2.0 * ORBIT_FREQ * self.state(i)[2]
            if f == 2:
                new = new - TIME_STEP * (2.0 - SHEAR_RATE) * ORBIT_FREQ * self.state(i)[1]
            return new
        if f == 4:
            ez, ey = self.edge(i, 2), self.edge(i, 1)
            curl = (up_y(ez) - ez) - (up_z(ey) - ey)
        elif f == 5:
            ex = self.edge(i, 0)
            curl = (up_z(ex) - ex) - (self.edge(i + 1, 2) - self.edge(i, 2))
        else:
            ex = self.edge(i, 0)
            curl = (self.edge(i + 1, 1) - self.edge(i, 1)) - (up_y(ex) - ex)
        return self.state(i)[f] - edge_step * curl


def pass_kernel(*refs):
    sources, targets, kept, sems = refs[:3], refs[3:6], refs[6:9], refs[9]
    inward = [pltpu.make_async_copy(src, dst, sems.at[0, k]) for k, (src, dst) in enumerate(zip(sources, kept))]
    outward = [pltpu.make_async_copy(src, dst, sems.at[1, k]) for k, (src, dst) in enumerate(zip(kept, targets))]
    for copy in inward:
        copy.start()
    for there, back in zip(inward, outward):
        there.wait()
        back.start()
    for copy in outward:
        copy.wait()


def body(density, momentum, field, shift, frac):
    hbm = pl.BlockSpec(memory_space=pl.ANY)
    f32 = jnp.float32
    shapes = tuple(jax.ShapeDtypeStruct(a.shape, f32) for a in (density, momentum, field))
    results = pl.pallas_call(
        step_kernel,
        out_shape=shapes,
        in_specs=[hbm] * 5,
        out_specs=(hbm,) * 3,
        scratch_shapes=[
            pltpu.SMEM(shift.shape, jnp.int32),
            pltpu.SMEM(frac.shape, f32),
            pltpu.VMEM(density.shape, f32),
            pltpu.VMEM(momentum.shape, f32),
            pltpu.VMEM(field.shape, f32),
            pltpu.VMEM((PARTS, RING, LANES), f32),
            pltpu.VMEM((PARTS, RING, LANES), f32),
            pltpu.VMEM((PARTS, RING, LANES), f32),
            pltpu.VMEM((2 * PHI, 8, LANES), f32),
            pltpu.VMEM((PHI, 8, LANES), f32),
            pltpu.VMEM((PARTS, RING, LANES), f32),
            pltpu.VMEM((2, 2, HALF, LANES), f32),
            pltpu.VMEM((2, 8, LANES), f32),
            pltpu.VMEM((2, 8, LANES), f32),
            pltpu.VMEM((FIELDS, 4, 2, NZ, LANES), f32),
            pltpu.SemaphoreType.DMA((5,)),
            pltpu.SemaphoreType.DMA((PARTS,)),
            pltpu.SemaphoreType.DMA((PARTS,)),
            pltpu.SemaphoreType.DMA((PARTS,)),
            pltpu.SemaphoreType.DMA((PARTS,)),
            pltpu.SemaphoreType.DMA((5,)),
            pltpu.SemaphoreType.DMA((5,)),
            pltpu.SemaphoreType.DMA((24,)),
        ],
        compiler_params=pltpu.CompilerParams(
            collective_id=0, has_side_effects=True, vmem_limit_bytes=56 * 2**20
        ),
        name="step",
    )(shift, frac, density, momentum, field)
    return pl.pallas_call(
        pass_kernel,
        out_shape=shapes,
        in_specs=[hbm] * 3,
        out_specs=(hbm,) * 3,
        scratch_shapes=[pltpu.VMEM(a.shape, f32) for a in shapes] + [pltpu.SemaphoreType.DMA((2, 3))],
        compiler_params=pltpu.CompilerParams(vmem_limit_bytes=56 * 2**20),
        name="hand_on",
    )(*results)


def solution(mesh):
    return jax.shard_map(
        body,
        mesh=mesh,
        in_specs=(
            P("row", None, "phi"),
            P(None, "row", None, "phi"),
            P(None, "row", None, "phi"),
            P("row"),
            P("row"),
        ),
        out_specs=(P("row", None, "phi"), P(None, "row", None, "phi"), P(None, "row", None, "phi")),
        check_vma=False,
    )
```

```python
import functools

import jax
import jax.numpy as jnp
from jax import lax
from jax.experimental import pallas as pl
from jax.experimental.pallas import tpu as pltpu
from jax.sharding import PartitionSpec as P

MESH = pl.DeviceIdType.MESH
TIME_STEP = 0.025
SOUND_SQUARED = 1.0
ORBIT_FREQ = 1.0
SHEAR_RATE = 1.5

ROWS = 8
PHI = 32
NZ = 16
LANES = 128
FIELDS = 7
PARTS = 4
COLUMNS = ((0, 3), (0, 3), (1, 2), (1, 2))
FIRST = (0, 4, 0, 4)
TILE = 8
RING = PHI * TILE
HALF = RING // 2
OUT_ROWS = (8, 8, 8, 6)
UPPER = (4, 4, 4, 3)
BACK_ROWS = (8, 8, 8, 7)


def after(values, by):
    return jnp.concatenate([values[by:], values[:by]], 0)


def ring_exit(q, fraction, lane, later, earlier):
    def upward(by):
        turned = pltpu.roll(q, LANES - by, 2)
        return jnp.where(lane >= LANES - by, later(turned), turned)

    def downward(values):
        turned = pltpu.roll(values, 1, 2)
        return jnp.where(lane == 0, earlier(turned), turned)

    one, two, before = upward(1), upward(2), downward(q)
    face = 7.0 / 12.0 * (q + one) - 1.0 / 12.0 * (before + two)
    face = jnp.clip(face, jnp.minimum(q, one), jnp.maximum(q, one))
    left = downward(face)
    curvature = 6.0 * (q - 0.5 * (face + left))
    outgoing = fraction * (
        face - 0.5 * fraction * (face - left - (1.0 - 2.0 / 3.0 * fraction) * curvature)
    )
    return q - outgoing + downward(outgoing)


def step_kernel(
    shift_hbm, frac_hbm, dens_hbm, mom_hbm, fld_hbm, dens_out, mom_out, fld_out,
    shift_ref, frac_ref, dens_ref, mom_ref, fld_ref, send_f, recv_f, send_b, turned, tails, own_ref, halo_ref,
    five, five_ref, weave, sem_in, sem_fs, sem_fr, sem_bs, sem_br, sem_xs, sem_xr, sem_out,
):
    row = lax.axis_index("row")
    me = lax.axis_index("phi")
    above = (lax.rem(row + 1, ROWS), me)
    below = (lax.rem(row + ROWS - 1, ROWS), me)
    barrier = pltpu.get_barrier_semaphore()

    def partner(i):
        k = i // 4
        dz = 4 + (k + 1) // 2 * (1 - 2 * (k % 2))
        z = lax.rem(me // 2 + dz + 8, 8)
        x = lax.rem(me // 16 + 1 - i // 2 % 2, 2)
        return x * 16 + z * 2 + lax.rem(me + 1 - i % 2, 2)

    def greet(i, carry):
        pl.semaphore_signal(
            barrier, inc=1, device_id=(row, partner(i)), device_id_type=MESH
        )
        return carry

    lax.fori_loop(0, PHI - 1, greet, 0, unroll=True)
    pl.semaphore_signal(barrier, inc=1, device_id=above, device_id_type=MESH)
    pl.semaphore_signal(barrier, inc=1, device_id=below, device_id_type=MESH)

    fetches = [
        pltpu.make_async_copy(src, dst, sem_in.at[k])
        for k, (src, dst) in enumerate((
            (dens_hbm, dens_ref), (mom_hbm, mom_ref), (fld_hbm, fld_ref),
            (shift_hbm, shift_ref), (frac_hbm, frac_ref),
        ))
    ]
    for fetch in fetches:
        fetch.start()

    def source(f, x, zs, ys):
        if f == 0:
            return dens_ref[x, zs, ys]
        if f < 4:
            return mom_ref[f - 1, x, zs, ys]
        return fld_ref[f - 4, x, zs, ys]

    def arrange(part):
        for side in range(2):
            for half in range(2):
                for zt in range(2):
                    for j in range(3 if part == 3 else 4):
                        f, x = FIRST[part] + j, COLUMNS[part][side]
                        if f == FIELDS:
                            f, x = 4, 1
                        block = source(
                            f, x, slice(8 * zt, 8 * zt + 8), slice(LANES * half, LANES * half + LANES)
                        )
                        first = (side * NZ + 8 * zt) * TILE + half * UPPER[part] + j
                        send_f[part, pl.ds(first, 8, stride=TILE), :] = block

    def rows_of(index, count=TILE):
        return pl.ds(pl.multiple_of(index * TILE, TILE), count)

    def spread(part, count, src, dst, send_sem, recv_sem):
        def one(i, carry):
            to = partner(i)
            pltpu.make_async_remote_copy(
                src_ref=src.at[part, rows_of(to, count), :],
                dst_ref=dst.at[part, rows_of(me, count), :],
                send_sem=send_sem.at[part],
                recv_sem=recv_sem.at[part],
                device_id=(row, to),
                device_id_type=MESH,
            ).start()
            return carry

        lax.fori_loop(0, PHI - 1, one, 0)

    def settle(part, count, buffer, sem):
        rows = buffer.at[part, pl.ds(0, (PHI - 1) * count), :]
        pltpu.make_async_copy(rows, rows, sem.at[part]).wait()

    def send_out(part):
        spread(part, OUT_ROWS[part], send_f, recv_f, sem_fs, sem_fr)

    lane = lax.broadcasted_iota(jnp.int32, (1, 8, LANES), 2)
    sub = lax.broadcasted_iota(jnp.int32, (1, 8, LANES), 1)
    lower = sub < 4
    spare = (sub & 3) == 3

    def later(values):
        return pltpu.roll(jnp.where(lower, after(values, 1), values), 4, 1)

    def earlier(values):
        return pltpu.roll(jnp.where(lower, values, after(values, -1)), 4, 1)

    def turn(part):
        settle(part, OUT_ROWS[part], recv_f, sem_fr)
        recv_f[part, rows_of(me), :] = send_f[part, rows_of(me), :]
        column = jnp.where(me < NZ, COLUMNS[part][0], COLUMNS[part][1])
        fraction = frac_ref[column]
        cells = shift_ref[column]
        inner = cells & (LANES - 1)
        if part == 1:
            fraction = jnp.where(spare, frac_ref[1], fraction)
            cells_1 = shift_ref[1]
            inner_1 = cells_1 & (LANES - 1)
        q = recv_f[part].reshape(PHI, 8, LANES)
        if part == 3:
            q = jnp.where(lower, q, pltpu.roll(q, 1, 1))
        exited = ring_exit(q, fraction, lane, later, earlier)
        rolled = pltpu.roll(exited, inner, 2)
        if part == 1:
            rolled = jnp.where(spare, pltpu.roll(exited, inner_1, 2), rolled)
        turned[0:PHI] = rolled
        turned[PHI:] = rolled

        def moved(amount):
            start = PHI - lax.shift_right_logical(amount, 8)
            blocks = jnp.stack([turned[start + j] for j in range(PHI)])
            return jnp.where((amount & LANES) == 0, blocks, earlier(blocks))

        out, split = moved(cells), inner
        if part == 1:
            out, split = jnp.where(spare, moved(cells_1), out), jnp.where(spare, inner_1, inner)
        out = jnp.where(lane >= split, out, earlier(out))
        ends = pltpu.roll(out, 1, 2)
        ends = jnp.where(lane == 0, pltpu.roll(after(ends, -1), 4, 1), after(ends, 1))
        spot = jnp.where(sub < (3 if part == 3 else 4), lane - 3 * (sub + FIRST[part]), -1)
        packed = jnp.where(spot == 0, ends[:, :, 0:1], 0.0)
        packed = jnp.where(spot == 1, ends[:, :, 1:2], packed)
        packed = jnp.where(spot == 2, ends[:, :, 2:3], packed)
        packed = jnp.sum(packed, axis=1, keepdims=True)
        if FIRST[part] == 0:
            tails[...] = jnp.broadcast_to(packed, tails.shape)
        else:
            packed = packed + tails[...]
            if part == 1:
                out = jnp.where((sub == 7) & (me < NZ), pltpu.roll(out, 4, 1), out)
            out = jnp.where(sub == 3, packed, out)
        send_b[part] = out.reshape(RING, LANES)
        spread(part, BACK_ROWS[part], send_b, own_ref, sem_bs, sem_br)
        own_ref[part, rows_of(me), :] = send_b[part, rows_of(me), :]

    def swap_of(k, src, dst, to):
        return pltpu.make_async_remote_copy(
            src_ref=src, dst_ref=dst, send_sem=sem_xs.at[k], recv_sem=sem_xr.at[k],
            device_id=to, device_id_type=MESH,
        )

    def swap(part):
        settle(part, BACK_ROWS[part], own_ref, sem_br)
        both = [
            swap_of(2 * part, own_ref.at[part, pl.ds(HALF, HALF), :], halo_ref.at[0, part], above),
            swap_of(2 * part + 1, own_ref.at[part, pl.ds(0, HALF), :], halo_ref.at[1, part], below),
        ]
        for each in both:
            each.start()
        return both

    fetches[0].wait()
    fetches[1].wait()
    arrange(0)
    pl.semaphore_wait(barrier, PHI - 1 + 2)
    send_out(0)
    for fetch in fetches[2:]:
        fetch.wait()
    arrange(1)
    send_out(1)
    arrange(2)
    send_out(2)
    arrange(3)
    turn(0)
    send_out(3)
    turn(1)
    turn(2)
    swaps = swap(0)
    turn(3)
    swaps += swap(1)
    for k in range(2):
        five[k] = own_ref[1, pl.ds(HALF + TILE * k + 7, 8, stride=2 * TILE), :]
    swaps.append(swap_of(4, five, five_ref, below))
    swaps[-1].start()

    def gather(rows, ends, f):
        pieces = []
        for k in range(2):
            halves = [part[pl.ds(base + k * TILE + r, 8, stride=2 * TILE), :] for part, base, r in rows]
            part, base = ends
            tail = part[pl.ds(base + k * TILE + 3, 8, stride=2 * TILE), :]
            pieces.append(
                jnp.concatenate(halves + [pltpu.roll(tail, LANES - (3 * f + 1), 1)], 1)[None]
            )
        return jnp.concatenate(pieces, 0)

    def load(i):
        if i in (-1, 4):
            parts, base = [halo_ref.at[0 if i < 0 else 1, k] for k in range(2)], 0
        else:
            parts = [own_ref.at[(0 if i in (0, 3) else 2) + k] for k in range(2)]
            base = 0 if i < 2 else HALF
        return [
            gather([(parts[f // 4], base, f % 4), (parts[f // 4], base, 4 + f % 4)], (parts[1], base), f)
            for f in range(FIELDS)
        ]

    def load_one():
        part = own_ref.at[1]
        return gather([(part, 0, 7), (part, HALF, 7)], (part, 0), FIELDS)

    def load_five():
        part = halo_ref.at[1, 1]
        pieces = []
        for k in range(2):
            lower_half = part[pl.ds(k * TILE + 7, 8, stride=2 * TILE), :]
            tail = part[pl.ds(k * TILE + 3, 8, stride=2 * TILE), :]
            pieces.append(
                jnp.concatenate([lower_half, five_ref[k], pltpu.roll(tail, LANES - 22, 1)], 1)[None]
            )
        return jnp.concatenate(pieces, 0)

    step = Step(load, {1: load_one, 5: load_five})
    writes = []

    def finish(i, fields):
        for f in fields:
            values = step.result(f, i)
            for side in range(2):
                for k in range(2):
                    weave[f, i, side, pl.ds(k, 8, stride=2), :] = values[
                        k, :, side * LANES:side * LANES + LANES
                    ]
        for side in range(2):
            ys = pl.ds(side * LANES, LANES)
            for src, dst in (
                (weave.at[0, i, side], dens_out.at[i, :, ys]),
                (weave.at[pl.ds(1, 3), i, side], mom_out.at[:, i, :, ys]),
                (weave.at[pl.ds(4, 3), i, side], fld_out.at[:, i, :, ys]),
            ):
                write = pltpu.make_async_copy(src, dst, sem_out.at[len(writes)])
                write.start()
                writes.append(write)

    step.flux(0, 1)
    step.flux(0, 2)
    step.side(3, 0)
    settle(2, BACK_ROWS[2], own_ref, sem_br)
    settle(3, BACK_ROWS[3], own_ref, sem_br)
    finish(1, range(FIELDS))
    for i in (2, 3):
        step.flux(i, 0)
    for i in (1, 2):
        step.flux(i, 1)
        step.flux(i, 2)
    for each in swaps:
        each.wait()
    for i in (2, 0, 3):
        finish(i, range(FIELDS))
    for part in range(PARTS):
        settle(part, OUT_ROWS[part], send_f, sem_fs)
        settle(part, BACK_ROWS[part], send_b, sem_bs)
    for write in writes:
        write.wait()


def up_z(values):
    return jnp.concatenate([values[1:2], pltpu.roll(values[0:1], 7, 1)], 0)


def low_z(values):
    return jnp.concatenate([pltpu.roll(values[1:2], 1, 1), values[0:1]], 0)


def up_y(values):
    return pltpu.roll(values, values.shape[2] - 1, 2)


def low_y(values):
    return pltpu.roll(values, 1, 2)


def same(values):
    return values


def main(values):
    return values[:, :, : 2 * LANES]


def face_flux(low, high, normal, n, moved, wanted, narrow):
    square = normal * normal

    def fast(side, shifted):
        return shifted(side["speed"]) + jnp.sqrt(shifted(side["base"]) + square * shifted(side["inv"]))

    fastest = jnp.maximum(fast(low, moved), fast(high, same))

    def blend(cut, flux, state):
        parts = (flux(low), flux(high), state(low), state(high))
        flux_low, flux_high, state_low, state_high = [
            moved(cut(part)) if k % 2 == 0 else cut(part) for k, part in enumerate(parts)
        ]
        return (flux_low + flux_high) - cut(fastest) * (state_high - state_low)

    def both(cut, value):
        return cut(normal) * (moved(cut(value(low))) + cut(value(high)))

    result = {}
    if "m" in wanted:
        cut = main if "m" in narrow else same
        result["m"] = [blend(cut, lambda side: side["m"][n], lambda side: side["rho"])]
        for t in range(3):
            if t == n:
                part = blend(cut, lambda side: side["push"], lambda side: side["m"][n]) - cut(square)
            else:
                part = blend(
                    cut, lambda side: side["m"][t] * side["v"][n], lambda side: side["m"][t]
                ) - both(cut, lambda side: side["b"][t])
            result["m"].append(part)
    for t in range(3):
        if t in wanted:
            cut = main if t in narrow else same
            result[t] = blend(
                cut, lambda side: side["b"][t] * side["v"][n], lambda side: side["b"][t]
            ) - both(cut, lambda side: side["v"][t])
    return result


class Step:
    def __init__(self, load, radial):
        self.load, self.radial, self.kept = load, radial, {}

    def keep(self, key, make):
        if key not in self.kept:
            self.kept[key] = make()
        return self.kept[key]

    def state(self, i):
        return self.keep(("state", i), lambda: self.load(i))

    def across(self, i, c):
        def make():
            faces = self.state(i)[4:]
            if c == 0:
                upper = self.radial[i + 1]() if i in (0, 4) else self.state(i + 1)[4]
            else:
                upper = up_y(faces[1]) if c == 1 else up_z(faces[2])
            return 0.5 * (faces[c] + upper)

        return self.keep(("across", i, c), make)

    def cell(self, i):
        def make():
            rho, mx, my, mz = self.state(i)[:4]
            inv = 1.0 / rho
            return dict(rho=rho, inv=inv, m=(mx, my, mz), v=(mx * inv, my * inv, mz * inv))

        return self.keep(("cell", i), make)

    def side(self, i, n):
        def make():
            cell = self.cell(i)
            t, u = [c for c in range(3) if c != n]
            b = {t: self.across(i, t), u: self.across(i, u)}
            if n == 2 and i in (-1, 4):
                cell, b = jax.tree.map(main, cell), jax.tree.map(main, b)
            square = b[t] * b[t] + b[u] * b[u]
            return dict(
                cell, b=b, base=SOUND_SQUARED + square * cell["inv"], speed=jnp.abs(cell["v"][n]),
                push=cell["m"][n] * cell["v"][n] + (cell["rho"] * SOUND_SQUARED + 0.5 * square),
            )

        return self.keep(("side", i, n), make)

    def flux(self, i, n):
        def make():
            inner = 0 <= i < 4
            normal = self.state(i)[4 + n]
            high = self.side(i, n)
            if n == 0:
                return face_flux(self.side(i - 1, 0), high, normal, 0, same, ("m", 1, 2), ("m", 2))
            wanted = ("m", 0, 3 - n) if inner else (0,)
            if n == 1:
                return face_flux(high, high, normal, 1, low_y, wanted, ())
            return face_flux(high, high, normal if inner else main(normal), 2, low_z, wanted, ("m", 0))

        return self.keep(("flux", i, n), make)

    def edge(self, i, c):
        def make():
            if c == 2:
                by = self.flux(i, 0)[1]
                return self.flux(i, 1)[0] + self.flux(i - 1, 1)[0] - (by + low_y(by))
            if c == 1:
                bz = self.flux(i, 0)[2]
                return bz + low_z(bz) - (self.flux(i, 2)[0] + self.flux(i - 1, 2)[0])
            by, bz = self.flux(i, 2)[1], self.flux(i, 1)[2]
            return by + low_y(by) - (bz + low_z(bz))

        return self.keep(("edge", i, c), make)

    def result(self, f, i):
        step, edge_step = 0.5 * TIME_STEP, 0.125 * TIME_STEP
        if f < 4:
            y, z = self.flux(i, 1)["m"][f], self.flux(i, 2)["m"][f]
            total = self.flux(i + 1, 0)["m"][f] - self.flux(i, 0)["m"][f]
            total = total + (main(up_y(y)) - main(y)) + (up_z(z) - z)
            new = main(self.state(i)[f]) - step * total
            if f == 1:
                new = new + TIME_STEP * 2.0 * ORBIT_FREQ * main(self.state(i)[2])
            if f == 2:
                new = new - TIME_STEP * (2.0 - SHEAR_RATE) * ORBIT_FREQ * main(self.state(i)[1])
            return new
        if f == 4:
            ez, ey = self.edge(i, 2), self.edge(i, 1)
            curl = (main(up_y(ez)) - main(ez)) - (up_z(ey) - ey)
        elif f == 5:
            ex = main(self.edge(i, 0))
            curl = (up_z(ex) - ex) - (main(self.edge(i + 1, 2)) - main(self.edge(i, 2)))
        else:
            ex = self.edge(i, 0)
            curl = (self.edge(i + 1, 1) - self.edge(i, 1)) - (main(up_y(ex)) - main(ex))
        return main(self.state(i)[f]) - edge_step * curl


def pass_kernel(*refs):
    sources, targets, kept, sems = refs[:3], refs[3:6], refs[6:9], refs[9]
    inward = [pltpu.make_async_copy(src, dst, sems.at[0, k]) for k, (src, dst) in enumerate(zip(sources, kept))]
    outward = [pltpu.make_async_copy(src, dst, sems.at[1, k]) for k, (src, dst) in enumerate(zip(kept, targets))]
    for copy in inward:
        copy.start()
    for there, back in zip(inward, outward):
        there.wait()
        back.start()
    for copy in outward:
        copy.wait()


def body(density, momentum, field, shift, frac):
    hbm = pl.BlockSpec(memory_space=pl.ANY)
    f32 = jnp.float32
    shapes = tuple(jax.ShapeDtypeStruct(a.shape, f32) for a in (density, momentum, field))
    results = pl.pallas_call(
        step_kernel,
        out_shape=shapes,
        in_specs=[hbm] * 5,
        out_specs=(hbm,) * 3,
        scratch_shapes=[
            pltpu.SMEM(shift.shape, jnp.int32),
            pltpu.SMEM(frac.shape, f32),
            pltpu.VMEM(density.shape, f32),
            pltpu.VMEM(momentum.shape, f32),
            pltpu.VMEM(field.shape, f32),
            pltpu.VMEM((PARTS, RING, LANES), f32),
            pltpu.VMEM((PARTS, RING, LANES), f32),
            pltpu.VMEM((PARTS, RING, LANES), f32),
            pltpu.VMEM((2 * PHI, 8, LANES), f32),
            pltpu.VMEM((PHI, 8, LANES), f32),
            pltpu.VMEM((PARTS, RING, LANES), f32),
            pltpu.VMEM((2, 2, HALF, LANES), f32),
            pltpu.VMEM((2, 8, LANES), f32),
            pltpu.VMEM((2, 8, LANES), f32),
            pltpu.VMEM((FIELDS, 4, 2, NZ, LANES), f32),
            pltpu.SemaphoreType.DMA((5,)),
            pltpu.SemaphoreType.DMA((PARTS,)),
            pltpu.SemaphoreType.DMA((PARTS,)),
            pltpu.SemaphoreType.DMA((PARTS,)),
            pltpu.SemaphoreType.DMA((PARTS,)),
            pltpu.SemaphoreType.DMA((5,)),
            pltpu.SemaphoreType.DMA((5,)),
            pltpu.SemaphoreType.DMA((24,)),
        ],
        compiler_params=pltpu.CompilerParams(
            collective_id=0, has_side_effects=True, vmem_limit_bytes=56 * 2**20
        ),
        name="step",
    )(shift, frac, density, momentum, field)
    return pl.pallas_call(
        pass_kernel,
        out_shape=shapes,
        in_specs=[hbm] * 3,
        out_specs=(hbm,) * 3,
        scratch_shapes=[pltpu.VMEM(a.shape, f32) for a in shapes] + [pltpu.SemaphoreType.DMA((2, 3))],
        compiler_params=pltpu.CompilerParams(vmem_limit_bytes=56 * 2**20),
        name="hand_on",
    )(*results)


def solution(mesh):
    return jax.shard_map(
        body,
        mesh=mesh,
        in_specs=(
            P("row", None, "phi"),
            P(None, "row", None, "phi"),
            P(None, "row", None, "phi"),
            P("row"),
            P("row"),
        ),
        out_specs=(P("row", None, "phi"), P(None, "row", None, "phi"), P(None, "row", None, "phi")),
        check_vma=False,
    )
```

```python
import functools

import jax
import jax.numpy as jnp
from jax import lax
from jax.experimental import pallas as pl
from jax.experimental.pallas import tpu as pltpu
from jax.sharding import PartitionSpec as P

MESH = pl.DeviceIdType.MESH
TIME_STEP = 0.025
SOUND_SQUARED = 1.0
ORBIT_FREQ = 1.0
SHEAR_RATE = 1.5

ROWS = 8
PHI = 32
NZ = 16
LANES = 128
FIELDS = 7
PARTS = 4
COLUMNS = ((0, 3), (0, 3), (1, 2), (1, 2))
FIRST = (0, 4, 0, 4)
TILE = 8
RING = PHI * TILE
HALF = RING // 2
OUT_ROWS = (8, 8, 8, 6)
UPPER = (4, 4, 4, 3)
BACK_ROWS = (8, 8, 8, 7)


def after(values, by):
    return jnp.concatenate([values[by:], values[:by]], 0)


def ring_exit(q, fraction, lane, later, earlier):
    def upward(by):
        turned = pltpu.roll(q, LANES - by, 2)
        return jnp.where(lane >= LANES - by, later(turned), turned)

    def downward(values):
        turned = pltpu.roll(values, 1, 2)
        return jnp.where(lane == 0, earlier(turned), turned)

    one, two, before = upward(1), upward(2), downward(q)
    face = 7.0 / 12.0 * (q + one) - 1.0 / 12.0 * (before + two)
    face = jnp.clip(face, jnp.minimum(q, one), jnp.maximum(q, one))
    left = downward(face)
    curvature = 6.0 * (q - 0.5 * (face + left))
    outgoing = fraction * (
        face - 0.5 * fraction * (face - left - (1.0 - 2.0 / 3.0 * fraction) * curvature)
    )
    return q - outgoing + downward(outgoing)


def step_kernel(
    shift_hbm, frac_hbm, dens_hbm, mom_hbm, fld_hbm, dens_out, mom_out, fld_out,
    shift_ref, frac_ref, dens_ref, mom_ref, fld_ref, send_f, recv_f, send_b, turned, tails, own_ref, halo_ref,
    five, five_ref, weave, sem_in, sem_fs, sem_fr, sem_bs, sem_br, sem_xs, sem_xr, sem_out,
):
    row = lax.axis_index("row")
    me = lax.axis_index("phi")
    above = (lax.rem(row + 1, ROWS), me)
    below = (lax.rem(row + ROWS - 1, ROWS), me)
    barrier = pltpu.get_barrier_semaphore()

    def partner(i):
        k = i // 4
        dz = 4 + (k + 1) // 2 * (1 - 2 * (k % 2))
        z = lax.rem(me // 2 + dz + 8, 8)
        x = lax.rem(me // 16 + 1 - i // 2 % 2, 2)
        return x * 16 + z * 2 + lax.rem(me + 1 - i % 2, 2)

    def greet(i, carry):
        pl.semaphore_signal(
            barrier, inc=1, device_id=(row, partner(i)), device_id_type=MESH
        )
        return carry

    lax.fori_loop(0, PHI - 1, greet, 0, unroll=True)
    pl.semaphore_signal(barrier, inc=1, device_id=above, device_id_type=MESH)
    pl.semaphore_signal(barrier, inc=1, device_id=below, device_id_type=MESH)

    fetches = [
        pltpu.make_async_copy(src, dst, sem_in.at[k])
        for k, (src, dst) in enumerate((
            (dens_hbm, dens_ref), (mom_hbm, mom_ref), (fld_hbm, fld_ref),
            (shift_hbm, shift_ref), (frac_hbm, frac_ref),
        ))
    ]
    for fetch in fetches:
        fetch.start()

    def source(f, x, zs, ys):
        if f == 0:
            return dens_ref[x, zs, ys]
        if f < 4:
            return mom_ref[f - 1, x, zs, ys]
        return fld_ref[f - 4, x, zs, ys]

    def arrange(part):
        for side in range(2):
            for half in range(2):
                for zt in range(2):
                    for j in range(3 if part == 3 else 4):
                        f, x = FIRST[part] + j, COLUMNS[part][side]
                        if f == FIELDS:
                            f, x = 4, 1
                        block = source(
                            f, x, slice(8 * zt, 8 * zt + 8), slice(LANES * half, LANES * half + LANES)
                        )
                        first = (side * NZ + 8 * zt) * TILE + half * UPPER[part] + j
                        send_f[part, pl.ds(first, 8, stride=TILE), :] = block

    def rows_of(index, count=TILE):
        return pl.ds(pl.multiple_of(index * TILE, TILE), count)

    def spread(part, count, src, dst, send_sem, recv_sem):
        def one(i, carry):
            to = partner(i)
            pltpu.make_async_remote_copy(
                src_ref=src.at[part, rows_of(to, count), :],
                dst_ref=dst.at[part, rows_of(me, count), :],
                send_sem=send_sem.at[part],
                recv_sem=recv_sem.at[part],
                device_id=(row, to),
                device_id_type=MESH,
            ).start()
            return carry

        lax.fori_loop(0, PHI - 1, one, 0)

    def settle(part, count, buffer, sem):
        rows = buffer.at[part, pl.ds(0, (PHI - 1) * count), :]
        pltpu.make_async_copy(rows, rows, sem.at[part]).wait()

    def send_out(part):
        spread(part, OUT_ROWS[part], send_f, recv_f, sem_fs, sem_fr)

    lane = lax.broadcasted_iota(jnp.int32, (1, 8, LANES), 2)
    sub = lax.broadcasted_iota(jnp.int32, (1, 8, LANES), 1)
    lower = sub < 4
    spare = (sub & 3) == 3

    def later(values):
        return pltpu.roll(jnp.where(lower, after(values, 1), values), 4, 1)

    def earlier(values):
        return pltpu.roll(jnp.where(lower, values, after(values, -1)), 4, 1)

    def turn(part):
        settle(part, OUT_ROWS[part], recv_f, sem_fr)
        recv_f[part, rows_of(me), :] = send_f[part, rows_of(me), :]
        column = jnp.where(me < NZ, COLUMNS[part][0], COLUMNS[part][1])
        fraction = frac_ref[column]
        cells = shift_ref[column]
        inner = cells & (LANES - 1)
        if part == 1:
            fraction = jnp.where(spare, frac_ref[1], fraction)
            cells_1 = shift_ref[1]
            inner_1 = cells_1 & (LANES - 1)
        q = recv_f[part].reshape(PHI, 8, LANES)
        if part == 3:
            q = jnp.where(lower, q, pltpu.roll(q, 1, 1))
        exited = ring_exit(q, fraction, lane, later, earlier)
        rolled = pltpu.roll(exited, inner, 2)
        if part == 1:
            rolled = jnp.where(spare, pltpu.roll(exited, inner_1, 2), rolled)
        turned[0:PHI] = rolled
        turned[PHI:] = rolled

        def moved(amount):
            start = PHI - lax.shift_right_logical(amount, 8)
            blocks = jnp.stack([turned[start + j] for j in range(PHI)])
            return jnp.where((amount & LANES) == 0, blocks, earlier(blocks))

        out, split = moved(cells), inner
        if part == 1:
            out, split = jnp.where(spare, moved(cells_1), out), jnp.where(spare, inner_1, inner)
        out = jnp.where(lane >= split, out, earlier(out))
        ends = pltpu.roll(out, 1, 2)
        ends = jnp.where(lane == 0, pltpu.roll(after(ends, -1), 4, 1), after(ends, 1))
        spot = jnp.where(sub < (3 if part == 3 else 4), lane - 3 * (sub + FIRST[part]), -1)
        packed = jnp.where(spot == 0, ends[:, :, 0:1], 0.0)
        packed = jnp.where(spot == 1, ends[:, :, 1:2], packed)
        packed = jnp.where(spot == 2, ends[:, :, 2:3], packed)
        packed = jnp.sum(packed, axis=1, keepdims=True)
        if FIRST[part] == 0:
            tails[...] = jnp.broadcast_to(packed, tails.shape)
        else:
            packed = packed + tails[...]
            if part == 1:
                out = jnp.where((sub == 7) & (me < NZ), pltpu.roll(out, 4, 1), out)
            out = jnp.where(sub == 3, packed, out)
        send_b[part] = out.reshape(RING, LANES)
        spread(part, BACK_ROWS[part], send_b, own_ref, sem_bs, sem_br)
        own_ref[part, rows_of(me), :] = send_b[part, rows_of(me), :]

    def swap_of(k, src, dst, to):
        return pltpu.make_async_remote_copy(
            src_ref=src, dst_ref=dst, send_sem=sem_xs.at[k], recv_sem=sem_xr.at[k],
            device_id=to, device_id_type=MESH,
        )

    def swap(part):
        settle(part, BACK_ROWS[part], own_ref, sem_br)
        both = [
            swap_of(2 * part, own_ref.at[part, pl.ds(HALF, HALF), :], halo_ref.at[0, part], above),
            swap_of(2 * part + 1, own_ref.at[part, pl.ds(0, HALF), :], halo_ref.at[1, part], below),
        ]
        for each in both:
            each.start()
        return both

    fetches[0].wait()
    fetches[1].wait()
    arrange(0)
    pl.semaphore_wait(barrier, PHI - 1 + 2)
    send_out(0)
    for fetch in fetches[2:]:
        fetch.wait()
    arrange(1)
    send_out(1)
    arrange(2)
    send_out(2)
    arrange(3)
    turn(0)
    send_out(3)
    turn(1)
    turn(2)
    swaps = swap(0)
    turn(3)
    swaps += swap(1)
    for k in range(2):
        five[k] = own_ref[1, pl.ds(HALF + TILE * k + 7, 8, stride=2 * TILE), :]
    swaps.append(swap_of(4, five, five_ref, below))
    swaps[-1].start()

    def gather(rows, ends, f):
        pieces = []
        for k in range(2):
            halves = [part[pl.ds(base + k * TILE + r, 8, stride=2 * TILE), :] for part, base, r in rows]
            part, base = ends
            tail = part[pl.ds(base + k * TILE + 3, 8, stride=2 * TILE), :]
            pieces.append(
                jnp.concatenate(halves + [pltpu.roll(tail, LANES - (3 * f + 1), 1)], 1)[None]
            )
        return jnp.concatenate(pieces, 0)

    def load(i):
        if i in (-1, 4):
            parts, base = [halo_ref.at[0 if i < 0 else 1, k] for k in range(2)], 0
        else:
            parts = [own_ref.at[(0 if i in (0, 3) else 2) + k] for k in range(2)]
            base = 0 if i < 2 else HALF
        return [
            gather([(parts[f // 4], base, f % 4), (parts[f // 4], base, 4 + f % 4)], (parts[1], base), f)
            for f in range(FIELDS)
        ]

    def load_one():
        part = own_ref.at[1]
        return gather([(part, 0, 7), (part, HALF, 7)], (part, 0), FIELDS)

    def load_five():
        part = halo_ref.at[1, 1]
        pieces = []
        for k in range(2):
            lower_half = part[pl.ds(k * TILE + 7, 8, stride=2 * TILE), :]
            tail = part[pl.ds(k * TILE + 3, 8, stride=2 * TILE), :]
            pieces.append(
                jnp.concatenate([lower_half, five_ref[k], pltpu.roll(tail, LANES - 22, 1)], 1)[None]
            )
        return jnp.concatenate(pieces, 0)

    step = Step(load, {1: load_one, 5: load_five})
    writes = []

    def put(i, fields):
        for f in fields:
            values = step.result(f, i)
            for side in range(2):
                for k in range(2):
                    weave[f, i, side, pl.ds(k, 8, stride=2), :] = values[
                        k, :, side * LANES:side * LANES + LANES
                    ]

    def write(i, first, count, dst):
        for side in range(2):
            ys = pl.ds(side * LANES, LANES)
            src = weave.at[pl.ds(first, count), i, side] if count > 1 else weave.at[first, i, side]
            copy = pltpu.make_async_copy(
                src, dst.at[:, i, :, ys] if count > 1 else dst.at[i, :, ys], sem_out.at[len(writes)]
            )
            copy.start()
            writes.append(copy)

    def finish(i, fields=range(FIELDS)):
        put(i, fields)
        if 0 in fields:
            write(i, 0, 1, dens_out)
            write(i, 1, 3, mom_out)
        if 6 in fields:
            write(i, 4, 3, fld_out)

    step.flux(0, 1)
    step.flux(0, 2)
    step.side(3, 0)
    settle(2, BACK_ROWS[2], own_ref, sem_br)
    settle(3, BACK_ROWS[3], own_ref, sem_br)
    finish(1, range(FIELDS))
    for i in (2, 3):
        step.flux(i, 0)
    for i in (1, 2):
        step.flux(i, 1)
        step.flux(i, 2)
    finish(2, range(5))
    for each in swaps:
        each.wait()
    finish(0)
    finish(3)
    finish(2, (5, 6))
    for part in range(PARTS):
        settle(part, OUT_ROWS[part], send_f, sem_fs)
        settle(part, BACK_ROWS[part], send_b, sem_bs)
    for copy in writes:
        copy.wait()


def up_z(values):
    return jnp.concatenate([values[1:2], pltpu.roll(values[0:1], 7, 1)], 0)


def low_z(values):
    return jnp.concatenate([pltpu.roll(values[1:2], 1, 1), values[0:1]], 0)


def up_y(values):
    return pltpu.roll(values, values.shape[2] - 1, 2)


def low_y(values):
    return pltpu.roll(values, 1, 2)


def same(values):
    return values


def main(values):
    return values[:, :, : 2 * LANES]


def face_flux(low, high, normal, n, moved, wanted, narrow):
    square = normal * normal

    def fast(side, shifted):
        return shifted(side["speed"]) + jnp.sqrt(shifted(side["base"]) + square * shifted(side["inv"]))

    fastest = jnp.maximum(fast(low, moved), fast(high, same))

    def blend(cut, flux, state):
        parts = (flux(low), flux(high), state(low), state(high))
        flux_low, flux_high, state_low, state_high = [
            moved(cut(part)) if k % 2 == 0 else cut(part) for k, part in enumerate(parts)
        ]
        return (flux_low + flux_high) - cut(fastest) * (state_high - state_low)

    def both(cut, value):
        return cut(normal) * (moved(cut(value(low))) + cut(value(high)))

    result = {}
    if "m" in wanted:
        cut = main if "m" in narrow else same
        result["m"] = [blend(cut, lambda side: side["m"][n], lambda side: side["rho"])]
        for t in range(3):
            if t == n:
                part = blend(cut, lambda side: side["push"], lambda side: side["m"][n]) - cut(square)
            else:
                part = blend(
                    cut, lambda side: side["m"][t] * side["v"][n], lambda side: side["m"][t]
                ) - both(cut, lambda side: side["b"][t])
            result["m"].append(part)
    for t in range(3):
        if t in wanted:
            cut = main if t in narrow else same
            result[t] = blend(
                cut, lambda side: side["b"][t] * side["v"][n], lambda side: side["b"][t]
            ) - both(cut, lambda side: side["v"][t])
    return result


class Step:
    def __init__(self, load, radial):
        self.load, self.radial, self.kept = load, radial, {}

    def keep(self, key, make):
        if key not in self.kept:
            self.kept[key] = make()
        return self.kept[key]

    def state(self, i):
        return self.keep(("state", i), lambda: self.load(i))

    def across(self, i, c):
        def make():
            faces = self.state(i)[4:]
            if c == 0:
                upper = self.radial[i + 1]() if i in (0, 4) else self.state(i + 1)[4]
            else:
                upper = up_y(faces[1]) if c == 1 else up_z(faces[2])
            return 0.5 * (faces[c] + upper)

        return self.keep(("across", i, c), make)

    def cell(self, i):
        def make():
            rho, mx, my, mz = self.state(i)[:4]
            inv = 1.0 / rho
            return dict(rho=rho, inv=inv, m=(mx, my, mz), v=(mx * inv, my * inv, mz * inv))

        return self.keep(("cell", i), make)

    def side(self, i, n):
        def make():
            cell = self.cell(i)
            t, u = [c for c in range(3) if c != n]
            b = {t: self.across(i, t), u: self.across(i, u)}
            if n == 2 and i in (-1, 4):
                cell, b = jax.tree.map(main, cell), jax.tree.map(main, b)
            square = b[t] * b[t] + b[u] * b[u]
            return dict(
                cell, b=b, base=SOUND_SQUARED + square * cell["inv"], speed=jnp.abs(cell["v"][n]),
                push=cell["m"][n] * cell["v"][n] + (cell["rho"] * SOUND_SQUARED + 0.5 * square),
            )

        return self.keep(("side", i, n), make)

    def flux(self, i, n):
        def make():
            inner = 0 <= i < 4
            normal = self.state(i)[4 + n]
            high = self.side(i, n)
            if n == 0:
                return face_flux(self.side(i - 1, 0), high, normal, 0, same, ("m", 1, 2), ("m", 2))
            wanted = ("m", 0, 3 - n) if inner else (0,)
            if n == 1:
                return face_flux(high, high, normal, 1, low_y, wanted, ())
            return face_flux(high, high, normal if inner else main(normal), 2, low_z, wanted, ("m", 0))

        return self.keep(("flux", i, n), make)

    def edge(self, i, c):
        def make():
            if c == 2:
                by = self.flux(i, 0)[1]
                return self.flux(i, 1)[0] + self.flux(i - 1, 1)[0] - (by + low_y(by))
            if c == 1:
                bz = self.flux(i, 0)[2]
                return bz + low_z(bz) - (self.flux(i, 2)[0] + self.flux(i - 1, 2)[0])
            by, bz = self.flux(i, 2)[1], self.flux(i, 1)[2]
            return by + low_y(by) - (bz + low_z(bz))

        return self.keep(("edge", i, c), make)

    def result(self, f, i):
        step, edge_step = 0.5 * TIME_STEP, 0.125 * TIME_STEP
        if f < 4:
            y, z = self.flux(i, 1)["m"][f], self.flux(i, 2)["m"][f]
            total = self.flux(i + 1, 0)["m"][f] - self.flux(i, 0)["m"][f]
            total = total + (main(up_y(y)) - main(y)) + (up_z(z) - z)
            new = main(self.state(i)[f]) - step * total
            if f == 1:
                new = new + TIME_STEP * 2.0 * ORBIT_FREQ * main(self.state(i)[2])
            if f == 2:
                new = new - TIME_STEP * (2.0 - SHEAR_RATE) * ORBIT_FREQ * main(self.state(i)[1])
            return new
        if f == 4:
            ez, ey = self.edge(i, 2), self.edge(i, 1)
            curl = (main(up_y(ez)) - main(ez)) - (up_z(ey) - ey)
        elif f == 5:
            ex = main(self.edge(i, 0))
            curl = (up_z(ex) - ex) - (main(self.edge(i + 1, 2)) - main(self.edge(i, 2)))
        else:
            ex = self.edge(i, 0)
            curl = (self.edge(i + 1, 1) - self.edge(i, 1)) - (main(up_y(ex)) - main(ex))
        return main(self.state(i)[f]) - edge_step * curl


def pass_kernel(*refs):
    sources, targets, kept, sems = refs[:3], refs[3:6], refs[6:9], refs[9]
    inward = [pltpu.make_async_copy(src, dst, sems.at[0, k]) for k, (src, dst) in enumerate(zip(sources, kept))]
    outward = [pltpu.make_async_copy(src, dst, sems.at[1, k]) for k, (src, dst) in enumerate(zip(kept, targets))]
    for copy in inward:
        copy.start()
    for there, back in zip(inward, outward):
        there.wait()
        back.start()
    for copy in outward:
        copy.wait()


def body(density, momentum, field, shift, frac):
    hbm = pl.BlockSpec(memory_space=pl.ANY)
    f32 = jnp.float32
    shapes = tuple(jax.ShapeDtypeStruct(a.shape, f32) for a in (density, momentum, field))
    results = pl.pallas_call(
        step_kernel,
        out_shape=shapes,
        in_specs=[hbm] * 5,
        out_specs=(hbm,) * 3,
        scratch_shapes=[
            pltpu.SMEM(shift.shape, jnp.int32),
            pltpu.SMEM(frac.shape, f32),
            pltpu.VMEM(density.shape, f32),
            pltpu.VMEM(momentum.shape, f32),
            pltpu.VMEM(field.shape, f32),
            pltpu.VMEM((PARTS, RING, LANES), f32),
            pltpu.VMEM((PARTS, RING, LANES), f32),
            pltpu.VMEM((PARTS, RING, LANES), f32),
            pltpu.VMEM((2 * PHI, 8, LANES), f32),
            pltpu.VMEM((PHI, 8, LANES), f32),
            pltpu.VMEM((PARTS, RING, LANES), f32),
            pltpu.VMEM((2, 2, HALF, LANES), f32),
            pltpu.VMEM((2, 8, LANES), f32),
            pltpu.VMEM((2, 8, LANES), f32),
            pltpu.VMEM((FIELDS, 4, 2, NZ, LANES), f32),
            pltpu.SemaphoreType.DMA((5,)),
            pltpu.SemaphoreType.DMA((PARTS,)),
            pltpu.SemaphoreType.DMA((PARTS,)),
            pltpu.SemaphoreType.DMA((PARTS,)),
            pltpu.SemaphoreType.DMA((PARTS,)),
            pltpu.SemaphoreType.DMA((5,)),
            pltpu.SemaphoreType.DMA((5,)),
            pltpu.SemaphoreType.DMA((24,)),
        ],
        compiler_params=pltpu.CompilerParams(
            collective_id=0, has_side_effects=True, vmem_limit_bytes=56 * 2**20
        ),
        name="step",
    )(shift, frac, density, momentum, field)
    return pl.pallas_call(
        pass_kernel,
        out_shape=shapes,
        in_specs=[hbm] * 3,
        out_specs=(hbm,) * 3,
        scratch_shapes=[pltpu.VMEM(a.shape, f32) for a in shapes] + [pltpu.SemaphoreType.DMA((2, 3))],
        compiler_params=pltpu.CompilerParams(vmem_limit_bytes=56 * 2**20),
        name="hand_on",
    )(*results)


def solution(mesh):
    return jax.shard_map(
        body,
        mesh=mesh,
        in_specs=(
            P("row", None, "phi"),
            P(None, "row", None, "phi"),
            P(None, "row", None, "phi"),
            P("row"),
            P("row"),
        ),
        out_specs=(P("row", None, "phi"), P(None, "row", None, "phi"), P(None, "row", None, "phi")),
        check_vma=False,
    )
```

```python
import functools

import jax
import jax.numpy as jnp
from jax import lax
from jax.experimental import pallas as pl
from jax.experimental.pallas import tpu as pltpu
from jax.sharding import PartitionSpec as P

MESH = pl.DeviceIdType.MESH
TIME_STEP = 0.025
SOUND_SQUARED = 1.0
ORBIT_FREQ = 1.0
SHEAR_RATE = 1.5

ROWS = 8
PHI = 32
NZ = 16
LANES = 128
FIELDS = 7
PARTS = 4
COLUMNS = ((0, 3), (0, 3), (1, 2), (1, 2))
FIRST = (0, 4, 0, 4)
TILE = 8
RING = PHI * TILE
HALF = RING // 2
OUT_ROWS = (8, 8, 8, 6)
UPPER = (4, 4, 4, 3)
BACK_ROWS = (8, 8, 8, 7)


def after(values, by):
    return jnp.concatenate([values[by:], values[:by]], 0)


def ring_exit(q, fraction, lane, later, earlier):
    def upward(by):
        turned = pltpu.roll(q, LANES - by, 2)
        return jnp.where(lane >= LANES - by, later(turned), turned)

    def downward(values):
        turned = pltpu.roll(values, 1, 2)
        return jnp.where(lane == 0, earlier(turned), turned)

    one, two, before = upward(1), upward(2), downward(q)
    face = 7.0 / 12.0 * (q + one) - 1.0 / 12.0 * (before + two)
    face = jnp.clip(face, jnp.minimum(q, one), jnp.maximum(q, one))
    left = downward(face)
    curvature = 6.0 * (q - 0.5 * (face + left))
    outgoing = fraction * (
        face - 0.5 * fraction * (face - left - (1.0 - 2.0 / 3.0 * fraction) * curvature)
    )
    return q - outgoing + downward(outgoing)


def step_kernel(
    shift_hbm, frac_hbm, dens_hbm, mom_hbm, fld_hbm, dens_out, mom_out, fld_out,
    shift_ref, frac_ref, dens_ref, mom_ref, fld_ref, send_f, recv_f, send_b, turned, tails, own_ref, halo_ref,
    five, five_ref, weave, sem_in, sem_fs, sem_fr, sem_bs, sem_br, sem_xs, sem_xr, sem_out,
):
    row = lax.axis_index("row")
    me = lax.axis_index("phi")
    above = (lax.rem(row + 1, ROWS), me)
    below = (lax.rem(row + ROWS - 1, ROWS), me)
    barrier = pltpu.get_barrier_semaphore()

    def partner(i):
        k = i % 16 // 2
        dz = 4 + (k + 1) // 2 * (1 - 2 * (k % 2))
        z = lax.rem(me // 2 + dz + 8, 8)
        x = lax.rem(me // 16 + 1 - i // 16, 2)
        return x * 16 + z * 2 + lax.rem(me + 1 - i % 2, 2)

    def greet(i, carry):
        pl.semaphore_signal(
            barrier, inc=1, device_id=(row, partner(i)), device_id_type=MESH
        )
        return carry

    lax.fori_loop(0, PHI - 1, greet, 0, unroll=True)
    pl.semaphore_signal(barrier, inc=1, device_id=above, device_id_type=MESH)
    pl.semaphore_signal(barrier, inc=1, device_id=below, device_id_type=MESH)

    fetches = [
        pltpu.make_async_copy(src, dst, sem_in.at[k])
        for k, (src, dst) in enumerate((
            (dens_hbm, dens_ref), (mom_hbm, mom_ref), (fld_hbm, fld_ref),
            (shift_hbm, shift_ref), (frac_hbm, frac_ref),
        ))
    ]
    for fetch in fetches:
        fetch.start()

    def source(f, x, zs, ys):
        if f == 0:
            return dens_ref[x, zs, ys]
        if f < 4:
            return mom_ref[f - 1, x, zs, ys]
        return fld_ref[f - 4, x, zs, ys]

    def arrange(part):
        for side in range(2):
            for half in range(2):
                for zt in range(2):
                    for j in range(3 if part == 3 else 4):
                        f, x = FIRST[part] + j, COLUMNS[part][side]
                        if f == FIELDS:
                            f, x = 4, 1
                        block = source(
                            f, x, slice(8 * zt, 8 * zt + 8), slice(LANES * half, LANES * half + LANES)
                        )
                        first = (side * NZ + 8 * zt) * TILE + half * UPPER[part] + j
                        send_f[part, pl.ds(first, 8, stride=TILE), :] = block

    def rows_of(index, count=TILE):
        return pl.ds(pl.multiple_of(index * TILE, TILE), count)

    def spread(part, count, src, dst, send_sem, recv_sem):
        def one(i, carry):
            to = partner(i)
            pltpu.make_async_remote_copy(
                src_ref=src.at[part, rows_of(to, count), :],
                dst_ref=dst.at[part, rows_of(me, count), :],
                send_sem=send_sem.at[part],
                recv_sem=recv_sem.at[part],
                device_id=(row, to),
                device_id_type=MESH,
            ).start()
            return carry

        lax.fori_loop(0, PHI - 1, one, 0)

    def settle(part, count, buffer, sem):
        rows = buffer.at[part, pl.ds(0, (PHI - 1) * count), :]
        pltpu.make_async_copy(rows, rows, sem.at[part]).wait()

    def send_out(part):
        spread(part, OUT_ROWS[part], send_f, recv_f, sem_fs, sem_fr)

    lane = lax.broadcasted_iota(jnp.int32, (1, 8, LANES), 2)
    sub = lax.broadcasted_iota(jnp.int32, (1, 8, LANES), 1)
    lower = sub < 4
    spare = (sub & 3) == 3

    def later(values):
        return pltpu.roll(jnp.where(lower, after(values, 1), values), 4, 1)

    def earlier(values):
        return pltpu.roll(jnp.where(lower, values, after(values, -1)), 4, 1)

    def turn(part):
        settle(part, OUT_ROWS[part], recv_f, sem_fr)
        recv_f[part, rows_of(me), :] = send_f[part, rows_of(me), :]
        column = jnp.where(me < NZ, COLUMNS[part][0], COLUMNS[part][1])
        fraction = frac_ref[column]
        cells = shift_ref[column]
        inner = cells & (LANES - 1)
        if part == 1:
            fraction = jnp.where(spare, frac_ref[1], fraction)
            cells_1 = shift_ref[1]
            inner_1 = cells_1 & (LANES - 1)
        q = recv_f[part].reshape(PHI, 8, LANES)
        if part == 3:
            q = jnp.where(lower, q, pltpu.roll(q, 1, 1))
        exited = ring_exit(q, fraction, lane, later, earlier)
        rolled = pltpu.roll(exited, inner, 2)
        if part == 1:
            rolled = jnp.where(spare, pltpu.roll(exited, inner_1, 2), rolled)
        turned[0:PHI] = rolled
        turned[PHI:] = rolled

        def moved(amount):
            start = PHI - lax.shift_right_logical(amount, 8)
            blocks = jnp.stack([turned[start + j] for j in range(PHI)])
            return jnp.where((amount & LANES) == 0, blocks, earlier(blocks))

        out, split = moved(cells), inner
        if part == 1:
            out, split = jnp.where(spare, moved(cells_1), out), jnp.where(spare, inner_1, inner)
        out = jnp.where(lane >= split, out, earlier(out))
        ends = pltpu.roll(out, 1, 2)
        ends = jnp.where(lane == 0, pltpu.roll(after(ends, -1), 4, 1), after(ends, 1))
        spot = jnp.where(sub < (3 if part == 3 else 4), lane - 3 * (sub + FIRST[part]), -1)
        packed = jnp.where(spot == 0, ends[:, :, 0:1], 0.0)
        packed = jnp.where(spot == 1, ends[:, :, 1:2], packed)
        packed = jnp.where(spot == 2, ends[:, :, 2:3], packed)
        packed = jnp.sum(packed, axis=1, keepdims=True)
        if FIRST[part] == 0:
            tails[...] = jnp.broadcast_to(packed, tails.shape)
        else:
            packed = packed + tails[...]
            if part == 1:
                out = jnp.where((sub == 7) & (me < NZ), pltpu.roll(out, 4, 1), out)
            out = jnp.where(sub == 3, packed, out)
        send_b[part] = out.reshape(RING, LANES)
        spread(part, BACK_ROWS[part], send_b, own_ref, sem_bs, sem_br)
        own_ref[part, rows_of(me), :] = send_b[part, rows_of(me), :]

    def swap_of(k, src, dst, to):
        return pltpu.make_async_remote_copy(
            src_ref=src, dst_ref=dst, send_sem=sem_xs.at[k], recv_sem=sem_xr.at[k],
            device_id=to, device_id_type=MESH,
        )

    def swap(part):
        settle(part, BACK_ROWS[part], own_ref, sem_br)
        both = [
            swap_of(2 * part, own_ref.at[part, pl.ds(HALF, HALF), :], halo_ref.at[0, part], above),
            swap_of(2 * part + 1, own_ref.at[part, pl.ds(0, HALF), :], halo_ref.at[1, part], below),
        ]
        for each in both:
            each.start()
        return both

    fetches[0].wait()
    fetches[1].wait()
    arrange(0)
    pl.semaphore_wait(barrier, PHI - 1 + 2)
    send_out(0)
    for fetch in fetches[2:]:
        fetch.wait()
    arrange(1)
    send_out(1)
    arrange(2)
    send_out(2)
    arrange(3)
    turn(0)
    send_out(3)
    turn(1)
    turn(2)
    swaps = swap(0)
    turn(3)
    swaps += swap(1)
    for k in range(2):
        five[k] = own_ref[1, pl.ds(HALF + TILE * k + 7, 8, stride=2 * TILE), :]
    swaps.append(swap_of(4, five, five_ref, below))
    swaps[-1].start()

    def gather(rows, ends, f):
        pieces = []
        for k in range(2):
            halves = [part[pl.ds(base + k * TILE + r, 8, stride=2 * TILE), :] for part, base, r in rows]
            part, base = ends
            tail = part[pl.ds(base + k * TILE + 3, 8, stride=2 * TILE), :]
            pieces.append(
                jnp.concatenate(halves + [pltpu.roll(tail, LANES - (3 * f + 1), 1)], 1)[None]
            )
        return jnp.concatenate(pieces, 0)

    def load(i):
        if i in (-1, 4):
            parts, base = [halo_ref.at[0 if i < 0 else 1, k] for k in range(2)], 0
        else:
            parts = [own_ref.at[(0 if i in (0, 3) else 2) + k] for k in range(2)]
            base = 0 if i < 2 else HALF
        return [
            gather([(parts[f // 4], base, f % 4), (parts[f // 4], base, 4 + f % 4)], (parts[1], base), f)
            for f in range(FIELDS)
        ]

    def load_one():
        part = own_ref.at[1]
        return gather([(part, 0, 7), (part, HALF, 7)], (part, 0), FIELDS)

    def load_five():
        part = halo_ref.at[1, 1]
        pieces = []
        for k in range(2):
            lower_half = part[pl.ds(k * TILE + 7, 8, stride=2 * TILE), :]
            tail = part[pl.ds(k * TILE + 3, 8, stride=2 * TILE), :]
            pieces.append(
                jnp.concatenate([lower_half, five_ref[k], pltpu.roll(tail, LANES - 22, 1)], 1)[None]
            )
        return jnp.concatenate(pieces, 0)

    step = Step(load, {1: load_one, 5: load_five})
    writes = []

    def put(i, fields):
        for f in fields:
            values = step.result(f, i)
            for side in range(2):
                for k in range(2):
                    weave[f, i, side, pl.ds(k, 8, stride=2), :] = values[
                        k, :, side * LANES:side * LANES + LANES
                    ]

    def write(i, first, count, dst):
        for side in range(2):
            ys = pl.ds(side * LANES, LANES)
            src = weave.at[pl.ds(first, count), i, side] if count > 1 else weave.at[first, i, side]
            copy = pltpu.make_async_copy(
                src, dst.at[:, i, :, ys] if count > 1 else dst.at[i, :, ys], sem_out.at[len(writes)]
            )
            copy.start()
            writes.append(copy)

    def finish(i, fields=range(FIELDS)):
        put(i, fields)
        if 0 in fields:
            write(i, 0, 1, dens_out)
            write(i, 1, 3, mom_out)
        if 6 in fields:
            write(i, 4, 3, fld_out)

    step.flux(0, 1)
    step.flux(0, 2)
    step.side(3, 0)
    settle(2, BACK_ROWS[2], own_ref, sem_br)
    settle(3, BACK_ROWS[3], own_ref, sem_br)
    finish(1, range(FIELDS))
    for i in (2, 3):
        step.flux(i, 0)
    for i in (1, 2):
        step.flux(i, 1)
        step.flux(i, 2)
    finish(2, range(5))
    for each in swaps:
        each.wait()
    finish(0)
    finish(3)
    finish(2, (5, 6))
    for part in range(PARTS):
        settle(part, OUT_ROWS[part], send_f, sem_fs)
        settle(part, BACK_ROWS[part], send_b, sem_bs)
    for copy in writes:
        copy.wait()


def up_z(values):
    return jnp.concatenate([values[1:2], pltpu.roll(values[0:1], 7, 1)], 0)


def low_z(values):
    return jnp.concatenate([pltpu.roll(values[1:2], 1, 1), values[0:1]], 0)


def up_y(values):
    return pltpu.roll(values, values.shape[2] - 1, 2)


def low_y(values):
    return pltpu.roll(values, 1, 2)


def same(values):
    return values


def main(values):
    return values[:, :, : 2 * LANES]


def face_flux(low, high, normal, n, moved, wanted, narrow):
    square = normal * normal

    def fast(side, shifted):
        return shifted(side["speed"]) + jnp.sqrt(shifted(side["base"]) + square * shifted(side["inv"]))

    fastest = jnp.maximum(fast(low, moved), fast(high, same))

    def blend(cut, flux, state):
        parts = (flux(low), flux(high), state(low), state(high))
        flux_low, flux_high, state_low, state_high = [
            moved(cut(part)) if k % 2 == 0 else cut(part) for k, part in enumerate(parts)
        ]
        return (flux_low + flux_high) - cut(fastest) * (state_high - state_low)

    def both(cut, value):
        return cut(normal) * (moved(cut(value(low))) + cut(value(high)))

    result = {}
    if "m" in wanted:
        cut = main if "m" in narrow else same
        result["m"] = [blend(cut, lambda side: side["m"][n], lambda side: side["rho"])]
        for t in range(3):
            if t == n:
                part = blend(cut, lambda side: side["push"], lambda side: side["m"][n]) - cut(square)
            else:
                part = blend(
                    cut, lambda side: side["m"][t] * side["v"][n], lambda side: side["m"][t]
                ) - both(cut, lambda side: side["b"][t])
            result["m"].append(part)
    for t in range(3):
        if t in wanted:
            cut = main if t in narrow else same
            result[t] = blend(
                cut, lambda side: side["b"][t] * side["v"][n], lambda side: side["b"][t]
            ) - both(cut, lambda side: side["v"][t])
    return result


class Step:
    def __init__(self, load, radial):
        self.load, self.radial, self.kept = load, radial, {}

    def keep(self, key, make):
        if key not in self.kept:
            self.kept[key] = make()
        return self.kept[key]

    def state(self, i):
        return self.keep(("state", i), lambda: self.load(i))

    def across(self, i, c):
        def make():
            faces = self.state(i)[4:]
            if c == 0:
                upper = self.radial[i + 1]() if i in (0, 4) else self.state(i + 1)[4]
            else:
                upper = up_y(faces[1]) if c == 1 else up_z(faces[2])
            return 0.5 * (faces[c] + upper)

        return self.keep(("across", i, c), make)

    def cell(self, i):
        def make():
            rho, mx, my, mz = self.state(i)[:4]
            inv = 1.0 / rho
            return dict(rho=rho, inv=inv, m=(mx, my, mz), v=(mx * inv, my * inv, mz * inv))

        return self.keep(("cell", i), make)

    def side(self, i, n):
        def make():
            cell = self.cell(i)
            t, u = [c for c in range(3) if c != n]
            b = {t: self.across(i, t), u: self.across(i, u)}
            if n == 2 and i in (-1, 4):
                cell, b = jax.tree.map(main, cell), jax.tree.map(main, b)
            square = b[t] * b[t] + b[u] * b[u]
            return dict(
                cell, b=b, base=SOUND_SQUARED + square * cell["inv"], speed=jnp.abs(cell["v"][n]),
                push=cell["m"][n] * cell["v"][n] + (cell["rho"] * SOUND_SQUARED + 0.5 * square),
            )

        return self.keep(("side", i, n), make)

    def flux(self, i, n):
        def make():
            inner = 0 <= i < 4
            normal = self.state(i)[4 + n]
            high = self.side(i, n)
            if n == 0:
                return face_flux(self.side(i - 1, 0), high, normal, 0, same, ("m", 1, 2), ("m", 2))
            wanted = ("m", 0, 3 - n) if inner else (0,)
            if n == 1:
                return face_flux(high, high, normal, 1, low_y, wanted, ())
            return face_flux(high, high, normal if inner else main(normal), 2, low_z, wanted, ("m", 0))

        return self.keep(("flux", i, n), make)

    def edge(self, i, c):
        def make():
            if c == 2:
                by = self.flux(i, 0)[1]
                return self.flux(i, 1)[0] + self.flux(i - 1, 1)[0] - (by + low_y(by))
            if c == 1:
                bz = self.flux(i, 0)[2]
                return bz + low_z(bz) - (self.flux(i, 2)[0] + self.flux(i - 1, 2)[0])
            by, bz = self.flux(i, 2)[1], self.flux(i, 1)[2]
            return by + low_y(by) - (bz + low_z(bz))

        return self.keep(("edge", i, c), make)

    def result(self, f, i):
        step, edge_step = 0.5 * TIME_STEP, 0.125 * TIME_STEP
        if f < 4:
            y, z = self.flux(i, 1)["m"][f], self.flux(i, 2)["m"][f]
            total = self.flux(i + 1, 0)["m"][f] - self.flux(i, 0)["m"][f]
            total = total + (main(up_y(y)) - main(y)) + (up_z(z) - z)
            new = main(self.state(i)[f]) - step * total
            if f == 1:
                new = new + TIME_STEP * 2.0 * ORBIT_FREQ * main(self.state(i)[2])
            if f == 2:
                new = new - TIME_STEP * (2.0 - SHEAR_RATE) * ORBIT_FREQ * main(self.state(i)[1])
            return new
        if f == 4:
            ez, ey = self.edge(i, 2), self.edge(i, 1)
            curl = (main(up_y(ez)) - main(ez)) - (up_z(ey) - ey)
        elif f == 5:
            ex = main(self.edge(i, 0))
            curl = (up_z(ex) - ex) - (main(self.edge(i + 1, 2)) - main(self.edge(i, 2)))
        else:
            ex = self.edge(i, 0)
            curl = (self.edge(i + 1, 1) - self.edge(i, 1)) - (main(up_y(ex)) - main(ex))
        return main(self.state(i)[f]) - edge_step * curl


def pass_kernel(*refs):
    sources, targets, kept, sems = refs[:3], refs[3:6], refs[6:9], refs[9]
    inward = [pltpu.make_async_copy(src, dst, sems.at[0, k]) for k, (src, dst) in enumerate(zip(sources, kept))]
    outward = [pltpu.make_async_copy(src, dst, sems.at[1, k]) for k, (src, dst) in enumerate(zip(kept, targets))]
    for copy in inward:
        copy.start()
    for there, back in zip(inward, outward):
        there.wait()
        back.start()
    for copy in outward:
        copy.wait()


def body(density, momentum, field, shift, frac):
    hbm = pl.BlockSpec(memory_space=pl.ANY)
    f32 = jnp.float32
    shapes = tuple(jax.ShapeDtypeStruct(a.shape, f32) for a in (density, momentum, field))
    results = pl.pallas_call(
        step_kernel,
        out_shape=shapes,
        in_specs=[hbm] * 5,
        out_specs=(hbm,) * 3,
        scratch_shapes=[
            pltpu.SMEM(shift.shape, jnp.int32),
            pltpu.SMEM(frac.shape, f32),
            pltpu.VMEM(density.shape, f32),
            pltpu.VMEM(momentum.shape, f32),
            pltpu.VMEM(field.shape, f32),
            pltpu.VMEM((PARTS, RING, LANES), f32),
            pltpu.VMEM((PARTS, RING, LANES), f32),
            pltpu.VMEM((PARTS, RING, LANES), f32),
            pltpu.VMEM((2 * PHI, 8, LANES), f32),
            pltpu.VMEM((PHI, 8, LANES), f32),
            pltpu.VMEM((PARTS, RING, LANES), f32),
            pltpu.VMEM((2, 2, HALF, LANES), f32),
            pltpu.VMEM((2, 8, LANES), f32),
            pltpu.VMEM((2, 8, LANES), f32),
            pltpu.VMEM((FIELDS, 4, 2, NZ, LANES), f32),
            pltpu.SemaphoreType.DMA((5,)),
            pltpu.SemaphoreType.DMA((PARTS,)),
            pltpu.SemaphoreType.DMA((PARTS,)),
            pltpu.SemaphoreType.DMA((PARTS,)),
            pltpu.SemaphoreType.DMA((PARTS,)),
            pltpu.SemaphoreType.DMA((5,)),
            pltpu.SemaphoreType.DMA((5,)),
            pltpu.SemaphoreType.DMA((24,)),
        ],
        compiler_params=pltpu.CompilerParams(
            collective_id=0, has_side_effects=True, vmem_limit_bytes=56 * 2**20
        ),
        name="step",
    )(shift, frac, density, momentum, field)
    return pl.pallas_call(
        pass_kernel,
        out_shape=shapes,
        in_specs=[hbm] * 3,
        out_specs=(hbm,) * 3,
        scratch_shapes=[pltpu.VMEM(a.shape, f32) for a in shapes] + [pltpu.SemaphoreType.DMA((2, 3))],
        compiler_params=pltpu.CompilerParams(vmem_limit_bytes=56 * 2**20),
        name="hand_on",
    )(*results)


def solution(mesh):
    return jax.shard_map(
        body,
        mesh=mesh,
        in_specs=(
            P("row", None, "phi"),
            P(None, "row", None, "phi"),
            P(None, "row", None, "phi"),
            P("row"),
            P("row"),
        ),
        out_specs=(P("row", None, "phi"), P(None, "row", None, "phi"), P(None, "row", None, "phi")),
        check_vma=False,
    )
```
